512 devices in a mesh: ctx: 16 (over y, z_hi, core), exp: 32 (over x, z_lo).
Axes of the slice: x: 4, y: 4, z: 16 (z_hi: 2, z_lo: 8; z = z_hi * 8 + z_lo), core: 2. Of those that a mesh axis runs over, the one named last changes fastest.
Arguments:
- queries: bfloat16 [16, 32, 64, 4096], P('ctx', 'exp'), may hold values from -90 to 90
- new_keys_values: bfloat16 [16, 32, 64, 512], P('ctx', 'exp'), may hold values from -4.5 to 4.5
- cached_keys_values: bfloat16 [16, 32, 64, 512], P('ctx', 'exp'), may hold values from -4.5 to 4.5
- residual: bfloat16 [16, 32, 64, 4096], P(None, 'exp', None, 'ctx'), may hold values from -17 to 17
- out_weight: bfloat16 [4096, 4096], P('exp', 'ctx'), may hold values from -0.1875 to 0.1875
- norm_gain: float32 [4096], P('ctx'), may hold values from 0.1 to 1.9
- routes: int32 [16, 32, 64, 8], P(None, 'exp'), may hold values from 0 to 127, as said below
- gates: float32 [16, 32, 64, 8], P(None, 'exp'), may hold values from 0.3 to 1
- w_gate_up: bfloat16 [32, 4096, 3072], P('exp', 'ctx'), may hold values from -0.125 to 0.125
- w_down: bfloat16 [32, 1536, 4096], P('exp', None, 'ctx'), may hold values from -0.15625 to 0.15625
Outputs:
- layer_out: bfloat16 [16, 32, 64, 4096], P(None, 'exp', None, 'ctx')
The draws below stay inside these ranges and needn't reach their ends.
Inputs may be any that keep to these rules, and one draw needn't show every extreme that they name: `routes`: each row names 8 different experts, at most one of them below 32. Among the rows that share the second index, an expert below 32 is named by at most 16 of them, and some expert by exactly 16.
All inputs are finite; a program needn't handle non-finite values.
Results may differ from the reference program's by a relative error of at most 0.02.
Values may be sent and summed in bfloat16 or wider, within the bound.
A program may use at most 64 MiB of HBM per device.

```python
import math
import jax
import jax.numpy as jnp
from jax import lax

D = 4096
QUERY_HEADS = 32
KEY_VALUE_HEADS = 2
HEAD_SIZE = 128
FF = 1536
EXPERTS = 128
TOP = 8
TOK_DEV = 64
PAST_PER_BLOCK = 64
GROUP_TOTAL = 16
HELD_COUNT = 32
NEW_TOKENS = 1024
PAST_PER_SEQ = 1024
TOKENS = 32768
CAP = 16


def token_major(values):
    shaped = values.reshape(HELD_COUNT, GROUP_TOTAL, TOK_DEV, values.shape[2])
    return jnp.transpose(shaped, (1, 0, 2, 3))


def shared_rows(key, strength):
    root_random_key = jax.random.fold_in(key, 0)
    token_rows = jnp.clip(jax.random.normal(root_random_key, (HELD_COUNT, NEW_TOKENS, 2 * KEY_VALUE_HEADS * HEAD_SIZE), jnp.float32), -4.0, 4.0)
    places = jnp.arange(NEW_TOKENS)
    paired = (places % 32 == 5).astype(jnp.float32)[None, :, None] * strength
    key_portion = token_rows[:, :, :KEY_VALUE_HEADS * HEAD_SIZE]
    key_portion = (1.0 - paired) * key_portion
    return jnp.concatenate([key_portion, token_rows[:, :, KEY_VALUE_HEADS * HEAD_SIZE:]], axis=2)


def draw_new_keys_values(key, part):
    strength = 0.0
    token_rows = shared_rows(key, strength)
    return token_major(token_rows).astype(jnp.bfloat16)


def draw_queries(key, part):
    key = jax.random.fold_in(key, 2)
    query = 2.0 * jnp.clip(jax.random.normal(key, (HELD_COUNT, NEW_TOKENS, QUERY_HEADS * HEAD_SIZE), jnp.float32), -4.0, 4.0)
    return token_major(query).astype(jnp.bfloat16)


def draw_residual(key, part):
    key = jax.random.fold_in(key, 3)
    first, second, third = jax.random.split(key, 3)
    random_noise = jnp.clip(jax.random.normal(first, (TOKENS, D), jnp.float32), -4.0, 4.0)
    row_level = jax.random.uniform(second, (TOKENS, 1), jnp.float32)
    column_level = jax.random.uniform(third, (1, D), jnp.float32)
    rising = jnp.arange(D, dtype=jnp.float32)[None, :] / D
    row_scale = jnp.exp(math.log(10.0) * row_level) / 3.16
    column_scale = jnp.exp(math.log(3.0) * rising + math.log(3.3) * column_level) / 15.0
    values = random_noise * row_scale * column_scale
    return values.reshape(GROUP_TOTAL, HELD_COUNT, TOK_DEV, D).astype(jnp.bfloat16)


def route_block(key):
    first, second, third, fourth, fifth = jax.random.split(key, 5)
    order = jax.random.permutation(first, HELD_COUNT)
    second_load = jax.random.randint(second, (), 1, CAP + 1)
    slots = jnp.arange(NEW_TOKENS)
    spread = 2 + (slots - CAP - second_load) % (HELD_COUNT - 2)
    picked = jnp.where(slots < CAP, 0, jnp.where(slots < CAP + second_load, 1, spread))
    resident_pick = order[picked]
    others_span = EXPERTS - HELD_COUNT
    stride = others_span // TOP
    offset = jax.random.randint(fourth, (NEW_TOKENS, 1), 0, others_span)
    leading = jnp.where(slots < NEW_TOKENS // 4, resident_pick, HELD_COUNT + offset[:, 0])
    others = HELD_COUNT + (offset + stride * jnp.arange(1, TOP)[None, :]) % others_span
    listed = jnp.concatenate([leading[:, None], others], axis=1)
    listed = listed[jax.random.permutation(third, NEW_TOKENS)]
    turn = jax.random.randint(fifth, (NEW_TOKENS, 1), 0, TOP)
    where_from = (jnp.arange(TOP)[None, :] - turn) % TOP
    return jnp.take_along_axis(listed, where_from, axis=1).astype(jnp.int32)


def draw_routes(key, part):
    key = jax.random.fold_in(key, 4)
    blocks = jax.vmap(lambda index: route_block(jax.random.fold_in(key, index)))(jnp.arange(HELD_COUNT))
    blocks = blocks.reshape(HELD_COUNT, GROUP_TOTAL, TOK_DEV, TOP)
    return jnp.transpose(blocks, (1, 0, 2, 3)).astype(jnp.int32)


def raised(values, stream_key, source, target, parts, factor):
    def block_of(dim):
        return (jnp.arange(values.shape[dim]) // (values.shape[dim] // parts)).reshape((-1,) + (1,) * (values.ndim - 1 - dim))

    near = jax.random.permutation(stream_key, parts)[block_of(target)]
    far = (block_of(target) + parts // 2) % parts
    return jnp.where((block_of(source) == near) | (block_of(source) == far), factor * values, values)


def levels(key, dims, shards, smallest, high):
    def one(position, blocks):
        steps = jax.random.uniform(jax.random.fold_in(jax.random.fold_in(key, 6), position), (blocks,), jnp.float32, smallest / len(shards), high / len(shards))
        return jnp.repeat(jnp.exp(steps), dims[position] // blocks).reshape((-1,) + (1,) * (len(dims) - position - 1))

    gain = one(*shards[0])
    for cut in shards[1:]:
        gain = gain * one(*cut)
    return gain


def centred(key, dims, scale, limit, pieces=(), kind=jnp.bfloat16):
    level = levels(key, dims, pieces, -0.22, 0.18) if pieces else 1.0
    values = jax.random.normal(key, dims, jnp.float32) * scale * level
    return jnp.minimum(jnp.maximum(values, -limit), limit).astype(kind)


def gaussian_with(rng, shape, width, bound, cuts, heavy, kind=jnp.bfloat16):
    values = width * jax.random.normal(rng, shape, jnp.float32)
    if cuts:
        values = values * levels(rng, shape, cuts, -0.22, 0.18)
    return jnp.clip(raised(values, jax.random.fold_in(rng, 3), *heavy), -bound, bound).astype(kind)


def setup_inputs(seed: int = 0) -> dict:
    splits = jax.random.split(jax.random.key(seed), 11)
    return {
        "queries": draw_queries(jax.random.fold_in(splits[10], 71), 0),
        "new_keys_values": draw_new_keys_values(jax.random.fold_in(splits[10], 71), 0),
        "cached_keys_values": centred(splits[2], (GROUP_TOTAL, HELD_COUNT, PAST_PER_BLOCK, 2 * KEY_VALUE_HEADS * HEAD_SIZE), 1.0, 4.5, ((0, 16), (1, 32))),
        "residual": draw_residual(jax.random.fold_in(splits[10], 71), 0),
        "out_weight": gaussian_with(splits[4], (QUERY_HEADS * HEAD_SIZE, D), (QUERY_HEADS * HEAD_SIZE) ** -0.5, 0.1875, ((0, 32), (1, 16)), (0, 1, 32, 2.75)),
        "norm_gain": jnp.clip(1.0 + 0.18 * jax.random.normal(splits[5], (D,), jnp.float32), 0.1, 1.9),
        "routes": draw_routes(jax.random.fold_in(splits[10], 71), 0),
        "gates": jnp.clip(0.3 + 0.7 * jax.random.uniform(splits[7], (GROUP_TOTAL, HELD_COUNT, TOK_DEV, TOP), jnp.float32) ** levels(splits[7], (GROUP_TOTAL, HELD_COUNT, TOK_DEV, TOP), ((1, 32),), -0.2, 0.2), 0.3, 1.0),
        "w_gate_up": gaussian_with(splits[8], (HELD_COUNT, D, 2 * FF), D ** -0.5, 0.125, ((0, 32), (1, 16)), (1, 2, 16, 2.0)),
        "w_down": centred(splits[9], (HELD_COUNT, FF, D), FF ** -0.5, 0.15625, ((0, 32), (2, 16))),
    }


NEG_FILL = -1e+30

def head_attention(query_head, key_head, value_head, visible):
    scores = jnp.dot(query_head.astype(jnp.float32), key_head.astype(jnp.float32).T, precision=lax.Precision.HIGHEST) * HEAD_SIZE ** (-0.5)
    row_max = lax.optimization_barrier(jnp.max(jnp.where(visible, scores, NEG_FILL), axis=1, keepdims=True))
    weights = jnp.where(visible, jnp.exp(scores - row_max), 0.0)
    rounded = lax.optimization_barrier(weights.astype(jnp.bfloat16)).astype(jnp.float32)
    numerator = jnp.dot(rounded, value_head.astype(jnp.float32), precision=lax.Precision.HIGHEST)
    return (numerator / lax.optimization_barrier(jnp.sum(weights, axis=1, keepdims=True))).astype(jnp.bfloat16)

def sequence_major(array):
    return jnp.transpose(array, (1, 0, 2, 3)).reshape(HELD_COUNT * NEW_TOKENS, array.shape[3])

def reference(queries, new_keys_values, cached_keys_values, residual, out_weight, norm_gain, routes, gates, w_gate_up, w_down):
    seq_query = jnp.transpose(queries, (1, 0, 2, 3)).reshape(HELD_COUNT, NEW_TOKENS, QUERY_HEADS, HEAD_SIZE)
    sequence_keys_values = jnp.transpose(new_keys_values, (1, 0, 2, 3)).reshape(HELD_COUNT, NEW_TOKENS, 2, KEY_VALUE_HEADS, HEAD_SIZE)
    sequence_cached = jnp.transpose(cached_keys_values, (1, 0, 2, 3)).reshape(HELD_COUNT, PAST_PER_SEQ, 2, KEY_VALUE_HEADS, HEAD_SIZE)
    seq_all = jnp.concatenate([sequence_cached, sequence_keys_values], axis=1)
    row_places = jnp.arange(NEW_TOKENS, dtype=jnp.int32)
    key_places = jnp.arange(PAST_PER_SEQ + NEW_TOKENS, dtype=jnp.int32) - PAST_PER_SEQ
    visible = row_places[:, None] >= key_places[None, :]
    group_extent = QUERY_HEADS // KEY_VALUE_HEADS

    def one_sequence(operands):
        query_rows, key_rows = operands

        def one_head(head):
            query_head = lax.dynamic_index_in_dim(query_rows, head, 1, keepdims=False)
            common_key_head = head // group_extent
            key_head = lax.dynamic_index_in_dim(key_rows[:, 0], common_key_head, 1, keepdims=False)
            value_head = lax.dynamic_index_in_dim(key_rows[:, 1], common_key_head, 1, keepdims=False)
            return head_attention(query_head, key_head, value_head, visible)
        heads_out = lax.map(one_head, jnp.arange(QUERY_HEADS, dtype=jnp.int32))
        return jnp.transpose(heads_out, (1, 0, 2)).reshape(NEW_TOKENS, QUERY_HEADS * HEAD_SIZE)
    attended = lax.map(one_sequence, (seq_query, seq_all)).reshape(TOKENS, QUERY_HEADS * HEAD_SIZE)
    projected = jnp.dot(attended.astype(jnp.float32), out_weight.astype(jnp.float32), precision=lax.Precision.HIGHEST)
    mixed = sequence_major(residual).astype(jnp.float32) + projected
    normed = (mixed * lax.rsqrt(lax.optimization_barrier(jnp.mean(mixed * mixed, axis=1, keepdims=True)) + 1e-06) * norm_gain[None, :]).astype(jnp.bfloat16)
    route_rows = sequence_major(routes)
    gate_rows = sequence_major(gates)
    resident = route_rows < HELD_COUNT
    has_expert = jnp.any(resident, axis=1)
    target = lax.optimization_barrier(jnp.sum(jnp.where(resident, route_rows, 0), axis=1)).astype(jnp.int32)
    target = jnp.where(has_expert, target, HELD_COUNT).astype(jnp.int32)
    gate_share = lax.optimization_barrier(jnp.sum(jnp.where(resident, gate_rows, 0.0), axis=1))
    padded = jnp.concatenate([normed, jnp.zeros((1, D), jnp.bfloat16)], axis=0)
    width_block = D // GROUP_TOTAL
    most_rows = HELD_COUNT * CAP

    def one_expert(operands):
        expert, gate_up, down_proj = operands
        chosen = jnp.nonzero(target == expert, size=most_rows, fill_value=TOKENS)[0].astype(jnp.int32)
        row_block = padded[chosen].astype(jnp.float32)
        gate_up_wide = gate_up.astype(jnp.float32)
        summed = jnp.zeros((most_rows, 2 * FF), jnp.float32)
        for piece_index in range(GROUP_TOTAL):
            partial_term = jnp.dot(row_block[:, piece_index * width_block:(piece_index + 1) * width_block], gate_up_wide[piece_index * width_block:(piece_index + 1) * width_block], precision=lax.Precision.HIGHEST)
            summed = summed + lax.optimization_barrier(partial_term.astype(jnp.bfloat16)).astype(jnp.float32)
        activated = (jax.nn.silu(summed[:, :FF]) * summed[:, FF:]).astype(jnp.bfloat16)
        out_rows = jnp.dot(activated.astype(jnp.float32), down_proj.astype(jnp.float32), precision=lax.Precision.HIGHEST).astype(jnp.bfloat16)
        return (chosen, out_rows)
    chosen, out_rows = lax.map(one_expert, (jnp.arange(HELD_COUNT, dtype=jnp.int32), w_gate_up, w_down))
    collected = jnp.zeros((TOKENS + 1, D), jnp.float32).at[chosen.reshape(-1)].set(out_rows.reshape(-1, D).astype(jnp.float32))[:TOKENS]
    result = (mixed + gate_share[:, None] * collected).astype(jnp.bfloat16)
    return jnp.transpose(result.reshape(HELD_COUNT, GROUP_TOTAL, TOK_DEV, D), (1, 0, 2, 3))
```

```python
import math

import jax
import jax.numpy as jnp
from jax import lax
from jax.experimental import pallas as pl
from jax.experimental.pallas import tpu as pltpu
from jax.sharding import PartitionSpec as P

D = 4096
HEADS = 32
KV_HEADS = 2
HEAD = 128
FF = 1536
HALF = FF // 2
EXT = 128
NY, NX, NZ = 4, 4, 8
CH = 4
NEG = -1e30
SCALE = HEAD ** (-0.5) * math.log2(math.e)
BF = jnp.bfloat16
F32 = jnp.float32
MESH = pl.DeviceIdType.MESH


class Place:
    def __init__(self):
        ctx = lax.axis_index("ctx")
        exp = lax.axis_index("exp")
        self.y = lax.div(ctx, 4)
        self.h = lax.rem(lax.div(ctx, 2), 2)
        self.c = lax.rem(ctx, 2)
        self.x = lax.div(exp, NZ)
        self.z = lax.rem(exp, NZ)
        self.ctx = ctx
        self.exp = exp

    def dev(self, y=None, h=None, c=None, x=None, z=None):
        y = self.y if y is None else y
        h = self.h if h is None else h
        c = self.c if c is None else c
        x = self.x if x is None else x
        z = self.z if z is None else z
        return ((y * 2 + h) * 2 + c, x * NZ + z)


def rem(a, n):
    return lax.rem(a + n, n)


def send(src, dst, ss, rs, dev):
    return pltpu.make_async_remote_copy(
        src_ref=src, dst_ref=dst, send_sem=ss, recv_sem=rs, device_id=dev, device_id_type=MESH
    )


def greet(devs):
    barrier = pltpu.get_barrier_semaphore()
    for dev in devs:
        pl.semaphore_signal(barrier, inc=1, device_id=dev, device_id_type=MESH)


def loop(n, body, start=0):
    lax.fori_loop(start, n, lambda i, _: (body(i), None)[1], None)


def front_kernel(
    q_ref, new_ref, past_ref, w_ref, res_ref, mixed_ref,
    kv, wb, att, psend, precv, s_ref,
    kv_s, kv_r, wz_s, wz_r, wx_s, wx_r, at_s, at_r, p_s, p_r,
):
    me = Place()
    mate = me.dev(h=1 - me.h)
    sib = me.dev(c=1 - me.c)
    ring = me.h * NZ + me.z

    def ring_dev(step):
        there = rem(ring + step, 2 * NZ)
        return me.dev(h=lax.div(there, NZ), z=lax.rem(there, NZ))

    right, left = ring_dev(1), ring_dev(-1)
    ys = [me.dev(y=rem(me.y + k, NY)) for k in (1, 2, 3)]
    xs = [me.dev(x=rem(me.x + k, NX)) for k in (1, 2, 3)]
    greet([mate, sib, right, left] + ys + xs)

    kv[0, me.ctx] = past_ref[...]
    kv[1, me.ctx] = new_ref[...]
    wb[me.h, me.exp] = w_ref[...]
    pl.semaphore_wait(pltpu.get_barrier_semaphore(), 10)

    def kv_copy(block, slot, dev):
        part = kv.at[:, block]
        return send(part, part, kv_s.at[slot], kv_r.at[block], dev)

    def blk(y, h, c):
        return (y * 2 + h) * 2 + c

    kv_copies = []

    def kv_go(block, slot, dev):
        copy = kv_copy(block, slot, dev)
        copy.start()
        kv_copies.append(copy)

    kv_go(me.ctx, 0, mate)
    for k in (1, 2, 3):
        kv_go(me.ctx, k, ys[k - 1])
    kv_go(me.ctx, 4, sib)

    def w_part(shard, x):
        return wb.at[lax.div(shard, NZ), x * NZ + lax.rem(shard, NZ)]

    def w_right(step):
        shard = rem(ring - step + 1, 2 * NZ)
        part = w_part(shard, me.x)
        return send(part, part, wz_s.at[0, step - 1], wz_r.at[shard], right)

    def w_left(step):
        shard = rem(ring + step - 1, 2 * NZ)
        part = w_part(shard, me.x)
        return send(part, part, wz_s.at[1, step - 1], wz_r.at[shard], left)

    def w_wait(shard):
        part = w_part(shard, me.x)
        send(part, part, wz_s.at[0, 0], wz_r.at[shard], right).wait_recv()

    def w_x(shard, k):
        part = w_part(shard, me.x)
        return send(part, part, wx_s.at[k - 1, shard], wx_r.at[k - 1, shard], xs[k - 1])

    def w_spread(shard):
        for k in (1, 3, 2):
            w_x(shard, k).start()

    def ring_step(step):
        w_right(step).start()

        @pl.when(step < NZ)
        def _():
            w_left(step).start()

        one = rem(ring - step, 2 * NZ)
        w_wait(one)
        w_spread(one)

        @pl.when(step < NZ)
        def _():
            other = rem(ring + step, 2 * NZ)
            w_wait(other)
            w_spread(other)

    w_spread(ring)
    loop(3, ring_step, 1)
    for k in (1, 2, 3):
        block = blk(rem(me.y - k, NY), me.h, me.c)
        kv_copy(block, 0, sib).wait_recv()
        kv_go(block, 4 + k, sib)
    loop(6, ring_step, 3)
    block = blk(me.y, 1 - me.h, me.c)
    kv_copy(block, 0, sib).wait_recv()
    for k in (1, 2, 3):
        kv_go(block, 7 + k, ys[k - 1])
    kv_go(block, 11, sib)
    loop(NZ + 1, ring_step, 6)
    for k in (1, 2, 3):
        block = blk(rem(me.y - k, NY), 1 - me.h, me.c)
        kv_copy(block, 0, sib).wait_recv()
        kv_go(block, 11 + k, sib)
    for y in range(NY):
        for h in range(2):
            kv_copy(blk(y, h, 1 - me.c), 0, sib).wait_recv()

    mine = me.y * 2 + me.c
    tok = q_ref.shape[1]
    keys = 512

    def att_copy(chunk, who, slot, dev):
        part = att.at[chunk, who]
        return send(part, part, at_s.at[chunk, slot], at_r.at[chunk, who], dev)

    def pass_on(chunk):
        for k in (1, 2, 3):
            who = rem(me.y - k, NY) * 2 + me.c
            att_copy(chunk, who, 0, sib).wait_recv()
            att_copy(chunk, who, 3 + k, sib).start()

    def attend(chunk):
        row = lax.broadcasted_iota(jnp.int32, (tok, keys), 0)
        col = lax.broadcasted_iota(jnp.int32, (tok, keys), 1)
        last = me.ctx * 64 + chunk * tok
        for g in range(KV_HEADS):
            per = HEADS // KV_HEADS
            q = jnp.concatenate(
                [q_ref[chunk, :, (g * per + i) * HEAD : (g * per + i + 1) * HEAD] for i in range(per)], axis=0
            )
            top = None
            for kt in range(4):
                k = kv[kt // 2, (kt % 2) * 8 : (kt % 2) * 8 + 8, :, g * HEAD : (g + 1) * HEAD].reshape(keys, HEAD)
                s = lax.dot_general(q, k, (((1,), (1,)), ((), ())), preferred_element_type=F32)
                if kt >= 2:
                    bias = jnp.where(col + (kt - 2) * keys <= row + last, 0.0, NEG)
                    s = (s.reshape(per, tok, keys) + bias[None]).reshape(per * tok, keys)
                s_ref[:, kt * keys : (kt + 1) * keys] = s
                m = jnp.max(s, axis=1, keepdims=True)
                top = m if top is None else jnp.maximum(top, m)
            total = None
            acc = None
            for kt in range(4):
                p = jnp.exp2((s_ref[:, kt * keys : (kt + 1) * keys] - top) * SCALE)
                v = kv[
                    kt // 2, (kt % 2) * 8 : (kt % 2) * 8 + 8, :, (KV_HEADS + g) * HEAD : (KV_HEADS + g + 1) * HEAD
                ].reshape(keys, HEAD)
                t = jnp.sum(p, axis=1, keepdims=True)
                o = jnp.dot(p.astype(BF), v, preferred_element_type=F32)
                total = t if total is None else total + t
                acc = o if acc is None else acc + o
            out = (acc / total).astype(BF)
            for i in range(per):
                att[chunk, mine, :, (g * per + i) * HEAD : (g * per + i + 1) * HEAD] = out[i * tok : (i + 1) * tok]
        for k in (1, 2, 3):
            att_copy(chunk, mine, k - 1, ys[k - 1]).start()
        att_copy(chunk, mine, 3, sib).start()

        @pl.when(chunk > 0)
        def _():
            pass_on(chunk - 1)

    loop(CH, attend)
    pass_on(CH - 1)

    def w_arrive(shard):
        for k in (1, 2, 3):
            part = w_part(shard, rem(me.x - k, NX))
            send(part, part, wx_s.at[k - 1, shard], wx_r.at[k - 1, shard], xs[k - 1]).wait_recv()

    loop(2 * NZ, w_arrive)

    def p_copy(chunk):
        return send(psend.at[chunk], precv.at[chunk], p_s.at[chunk], p_r.at[chunk], mate)

    def rows_of(chunk):
        return att[chunk].reshape(8 * tok, D)

    def for_mate(chunk):
        for y in range(NY):
            att_copy(chunk, y * 2 + 1 - me.c, 0, sib).wait_recv()
        w = wb[1 - me.h].reshape(D, 256)
        psend[chunk] = jnp.dot(rows_of(chunk), w, preferred_element_type=F32).astype(BF)
        p_copy(chunk).start()

    loop(CH, for_mate)

    def place(chunk, half, value):
        for j in range(8):
            block = (j // 2) * 4 + half * 2 + j % 2
            mixed_ref[block, chunk] = res_ref[block, chunk].astype(F32) + value[j * tok : (j + 1) * tok].astype(F32)

    def for_me(chunk):
        w = wb[me.h].reshape(D, 256)
        place(chunk, me.h, jnp.dot(rows_of(chunk), w, preferred_element_type=F32))

    loop(CH, for_me)

    def from_mate(chunk):
        p_copy(chunk).wait_recv()
        place(chunk, 1 - me.h, precv[chunk])

    loop(CH, from_mate)

    for copy in kv_copies:
        copy.wait_send()

    def ring_left(step):
        w_right(step).wait_send()

        @pl.when(step < NZ)
        def _():
            w_left(step).wait_send()

    loop(NZ + 1, ring_left, 1)

    def x_left(shard):
        for k in (1, 2, 3):
            w_x(shard, k).wait_send()

    loop(2 * NZ, x_left)

    def att_left(chunk):
        for slot in range(7):
            att_copy(chunk, mine, slot, sib).wait_send()
        p_copy(chunk).wait_send()

    loop(CH, att_left)


def front(queries, new, past, w, res):
    sem = pltpu.SemaphoreType.DMA
    return pl.pallas_call(
        front_kernel,
        out_shape=jax.ShapeDtypeStruct((16, CH, 16, 256), F32),
        in_specs=[pl.BlockSpec(memory_space=pltpu.VMEM)] * 5,
        out_specs=pl.BlockSpec(memory_space=pltpu.VMEM),
        scratch_shapes=[
            pltpu.VMEM((2, 16, 64, 512), BF),
            pltpu.VMEM((2, 32, 128, 256), BF),
            pltpu.VMEM((CH, 8, 16, D), BF),
            pltpu.VMEM((CH, 128, 256), BF),
            pltpu.VMEM((CH, 128, 256), BF),
            pltpu.VMEM((256, 2048), F32),
            sem((15,)), sem((16,)),
            sem((2, 8)), sem((16,)),
            sem((3, 16)), sem((3, 16)),
            sem((CH, 7)), sem((CH, 8)),
            sem((CH,)), sem((CH,)),
        ],
        compiler_params=pltpu.CompilerParams(
            collective_id=0, has_side_effects=True, vmem_limit_bytes=48 * 2**20
        ),
        name="front",
    )(queries, new, past, w, res)


def pieces(column, rows):
    lane = lax.broadcasted_iota(jnp.int32, (rows, EXT), 1)
    wide = jnp.broadcast_to(column, (rows, EXT))
    high = wide.astype(BF).astype(F32)
    rest = wide - high
    middle = rest.astype(BF).astype(F32)
    low = rest - middle
    out = jnp.where(lane == 0, high, jnp.where(lane == 1, middle, jnp.where(lane == 2, low, 0.0)))
    return out.astype(BF)


def expert_kernel(
    mixed_ref, gain_ref, routes_ref, gates_ref, gu_ref, wd_ref, out_ref,
    gains, wgs, disp, arr, sarr, pb, yr, zb, zr, act, eo, rb, place_ref, share_ref,
    c_s, c_r, d_s, d_r, a_s, a_r, y_s, y_r, z_s, z_r, az_s, az_r, ay_s, ay_r, ac_s, ac_r, e_s, e_r,
):
    me = Place()
    mate = me.dev(h=1 - me.h)
    sib = me.dev(c=1 - me.c)
    ys = [me.dev(y=rem(me.y + k, NY)) for k in (1, 2, 3)]
    barrier = pltpu.get_barrier_semaphore()
    greet([mate, sib] + ys)

    def peer(o):
        x = rem(me.x + lax.div(o, NZ), NX)
        z = rem(me.z + lax.rem(o, NZ), NZ)
        return x * NZ + z

    def peer_dev(e):
        return (me.ctx, e)

    def hello(o):
        pl.semaphore_signal(barrier, inc=1, device_id=peer_dev(peer(o)), device_id_type=MESH)

    loop(NX * NZ, hello, 1)

    toks = routes_ref.shape[0]
    routes = routes_ref[...]
    held = routes < NX * NZ
    target = jnp.sum(jnp.where(held, routes, 0), axis=1, keepdims=True)
    has = jnp.sum(jnp.where(held, 1, 0), axis=1, keepdims=True)
    share_ref[...] = jnp.sum(jnp.where(held, gates_ref[...], 0.0), axis=1, keepdims=True)
    lane = lax.broadcasted_iota(jnp.int32, (toks, 128), 1)
    named = jnp.where(has > 0, target, -1)
    hot = jnp.where(lane == named, 1.0, 0.0)
    step = 128
    seen = jnp.zeros((1, 128), F32)
    tri = jnp.where(
        lax.broadcasted_iota(jnp.int32, (step, step), 1) < lax.broadcasted_iota(jnp.int32, (step, step), 0), 1.0, 0.0
    ).astype(BF)
    slot = lax.broadcasted_iota(jnp.int32, (step, 512), 1)
    for t in range(toks // step):
        part = hot[t * step : (t + 1) * step]
        before = jnp.dot(tri, part.astype(BF), preferred_element_type=F32) + seen
        at = jnp.sum(before * part, axis=1, keepdims=True).astype(jnp.int32)
        here = named[t * step : (t + 1) * step]
        index = jnp.where(here >= 0, here * 16 + at, -1)
        place_ref[t * step : (t + 1) * step] = jnp.where(slot == index, 1.0, 0.0).astype(BF)
        seen = seen + jnp.sum(part, axis=0, keepdims=True)

    gains[me.c] = jnp.broadcast_to(gain_ref[...], (8, 256))
    rows = (mixed_ref[...].reshape(toks, 256) * gain_ref[...]).astype(BF)
    picked = lax.dot_general(place_ref[...], rows, (((0,), (0,)), ((), ())), preferred_element_type=F32)
    disp[...] = picked.astype(BF).reshape(32, 16, 256)
    arr[me.exp] = disp[me.exp]
    pl.semaphore_wait(barrier, 36)

    def d_copy(o):
        e = peer(o)
        return send(disp.at[e], arr.at[me.exp], d_s.at[o], d_r.at[me.exp], peer_dev(e))

    loop(NX * NZ, lambda o: d_copy(o).start(), 1)

    theirs = pl.multiple_of((1 - me.c) * HALF, 128)
    c_copies = [
        send(gu_ref.at[:, pl.ds(theirs, HALF)], wgs.at[:, pl.ds(0, HALF)], c_s.at[0], c_r.at[0], sib),
        send(gu_ref.at[:, pl.ds(theirs + FF, HALF)], wgs.at[:, pl.ds(HALF, HALF)], c_s.at[1], c_r.at[1], sib),
        send(gains.at[me.c], gains.at[me.c], c_s.at[2], c_r.at[2], sib),
    ]
    for copy in c_copies:
        copy.start()

    def src_x(q):
        return rem(me.x - q, NX)

    def a_copy(q):
        x = src_x(q)
        part = arr.at[pl.ds(x * NZ, NZ)]
        return send(part, sarr.at[pl.ds(x * NZ, NZ)], a_s.at[x], a_r.at[x], sib)

    def collect(q):
        x = src_x(q)

        def one(z):
            e = x * NZ + z

            @pl.when(e != me.exp)
            def _():
                send(disp.at[0], arr.at[e], d_s.at[0], d_r.at[e], sib).wait_recv()

        loop(NZ, one)
        a_copy(q).start()

    loop(CH, collect)
    c_copies[0].wait_recv()
    c_copies[1].wait_recv()
    send(gains.at[me.c], gains.at[1 - me.c], c_s.at[2], c_r.at[2], sib).wait_recv()
    ours = pl.multiple_of(me.c * HALF, 128)

    def y_copy(q, k):
        there = rem(me.y + k, NY)
        part = pb.at[q, pl.ds(there * 32, 32)]
        return send(part, yr.at[q, k - 1], y_s.at[q, k - 1], y_r.at[q, k - 1], ys[k - 1])

    def gate_up(q):
        x = src_x(q)
        a_copy(q).wait_recv()
        mine = arr[pl.ds(x * NZ, NZ)].reshape(128, 256)
        other = sarr[pl.ds(x * NZ, NZ)].reshape(128, 256)
        a = mine.astype(F32) / gains[me.c, 0:1]
        b = other.astype(F32) / gains[1 - me.c, 0:1]
        squares = jnp.sum(a * a, axis=1, keepdims=True) + jnp.sum(b * b, axis=1, keepdims=True)
        pb[q, :, FF * 1 :] = pieces(squares, 128)
        gate = jnp.dot(mine, gu_ref[:, pl.ds(ours, HALF)], preferred_element_type=F32)
        gate += jnp.dot(other, wgs[:, 0:HALF], preferred_element_type=F32)
        pb[q, :, 0:HALF] = gate.astype(BF)
        up = jnp.dot(mine, gu_ref[:, pl.ds(ours + FF, HALF)], preferred_element_type=F32)
        up += jnp.dot(other, wgs[:, HALF:FF], preferred_element_type=F32)
        pb[q, :, HALF:FF] = up.astype(BF)
        for k in (1, 2, 3):
            y_copy(q, k).start()

    loop(CH, gate_up)

    def z_copy(q):
        part = zb.at[q, pl.ds((1 - me.h) * 16, 16)]
        return send(part, zr.at[q], z_s.at[q], z_r.at[q], mate)

    def y_sum(q):
        total = pb[q, pl.ds(pl.multiple_of(me.y * 32, 32), 32)].astype(F32)
        for k in (1, 2, 3):
            y_copy(q, k).wait_recv()
            total = total + yr[q, k - 1].astype(F32)
        zb[q, :, 0:FF] = total[:, 0:FF].astype(BF)
        zb[q, :, FF:] = pieces(jnp.sum(total[:, FF:], axis=1, keepdims=True), 32)
        z_copy(q).start()

    loop(CH, y_sum)

    def az_copy(q):
        part = act.at[q, me.c, me.y, me.h]
        return send(part, part, az_s.at[q], az_r.at[q], mate)

    def activate(q):
        z_copy(q).wait_recv()
        total = zb[q, pl.ds(pl.multiple_of(me.h * 16, 16), 16)].astype(F32) + zr[q].astype(F32)
        squares = jnp.sum(total[:, FF:], axis=1, keepdims=True)
        scale = lax.rsqrt(squares / D + 1e-6)
        gate = total[:, 0:HALF] * scale
        up = total[:, HALF:FF] * scale
        act[q, me.c, me.y, me.h] = (gate / (1.0 + jnp.exp(-gate)) * up).astype(BF)
        az_copy(q).start()

    loop(CH, activate)

    def ay_copy(q, y, k):
        part = act.at[q, me.c, y]
        return send(part, part, ay_s.at[q, k - 1], ay_r.at[q, y], ys[k - 1])

    def spread(q):
        part = act.at[q, me.c, me.y, 1 - me.h]
        send(part, part, az_s.at[q], az_r.at[q], mate).wait_recv()
        for k in (1, 2, 3):
            ay_copy(q, me.y, k).start()

    loop(CH, spread)

    def ac_copy(q, c):
        part = act.at[q, c]
        return send(part, part, ac_s.at[q], ac_r.at[q], sib)

    def share(q):
        for k in (1, 2, 3):
            ay_copy(q, rem(me.y - k, NY), k).wait_recv()
        ac_copy(q, me.c).start()

    loop(CH, share)

    def e_copy(o):
        e = peer(o)
        return send(eo.at[e], rb.at[me.exp], e_s.at[o], e_r.at[me.exp], peer_dev(e))

    def down(q):
        x = src_x(q)
        ac_copy(q, 1 - me.c).wait_recv()
        value = jnp.dot(act[q, 0].reshape(128, HALF), wd_ref[0:HALF], preferred_element_type=F32)
        value += jnp.dot(act[q, 1].reshape(128, HALF), wd_ref[HALF:FF], preferred_element_type=F32)
        eo[pl.ds(x * NZ, NZ)] = value.astype(BF).reshape(NZ, 16, 256)

        def back(z):
            o = rem(NX - q, NX) * NZ + z

            @pl.when(o != 0)
            def _():
                e_copy(o).start()

        loop(NZ, back)

    loop(CH, down)
    rb[me.exp] = eo[me.exp]

    def home(e):
        @pl.when(e != me.exp)
        def _():
            send(eo.at[0], rb.at[e], e_s.at[0], e_r.at[e], sib).wait_recv()

    loop(NX * NZ, home)
    back = rb[...].reshape(512, 256)
    for t in range(4):
        got = jnp.dot(place_ref[t * 256 : (t + 1) * 256], back, preferred_element_type=F32)
        value = mixed_ref[t * 4 : (t + 1) * 4].reshape(256, 256) + share_ref[t * 256 : (t + 1) * 256] * got
        out_ref[t * 4 : (t + 1) * 4] = value.astype(BF).reshape(4, 64, 256)

    for copy in c_copies:
        copy.wait_send()

    def peers_left(o):
        d_copy(o).wait_send()
        e_copy(o).wait_send()

    loop(NX * NZ, peers_left, 1)

    def chunk_left(q):
        a_copy(q).wait_send()
        z_copy(q).wait_send()
        az_copy(q).wait_send()
        ac_copy(q, me.c).wait_send()
        for k in (1, 2, 3):
            y_copy(q, k).wait_send()
            ay_copy(q, me.y, k).wait_send()

    loop(CH, chunk_left)


def experts(mixed, gain, routes, gates, gu, wd):
    sem = pltpu.SemaphoreType.DMA
    wide = FF + EXT
    return pl.pallas_call(
        expert_kernel,
        out_shape=jax.ShapeDtypeStruct((16, 64, 256), BF),
        in_specs=[pl.BlockSpec(memory_space=pltpu.VMEM)] * 6,
        out_specs=pl.BlockSpec(memory_space=pltpu.VMEM),
        scratch_shapes=[
            pltpu.VMEM((2, 8, 256), F32),
            pltpu.VMEM((256, FF), BF),
            pltpu.VMEM((32, 16, 256), BF),
            pltpu.VMEM((32, 16, 256), BF),
            pltpu.VMEM((32, 16, 256), BF),
            pltpu.VMEM((CH, 128, wide), BF),
            pltpu.VMEM((CH, 3, 32, wide), BF),
            pltpu.VMEM((CH, 32, wide), BF),
            pltpu.VMEM((CH, 16, wide), BF),
            pltpu.VMEM((CH, 2, NY, 2, 16, HALF), BF),
            pltpu.VMEM((32, 16, 256), BF),
            pltpu.VMEM((32, 16, 256), BF),
            pltpu.VMEM((1024, 512), BF),
            pltpu.VMEM((1024, 1), F32),
            sem((3,)), sem((3,)),
            sem((32,)), sem((32,)),
            sem((4,)), sem((4,)),
            sem((CH, 3)), sem((CH, 3)),
            sem((CH,)), sem((CH,)),
            sem((CH,)), sem((CH,)),
            sem((CH, 3)), sem((CH, NY)),
            sem((CH,)), sem((CH,)),
            sem((32,)), sem((32,)),
        ],
        compiler_params=pltpu.CompilerParams(
            collective_id=1, has_side_effects=True, vmem_limit_bytes=48 * 2**20
        ),
        name="experts",
    )(mixed, gain, routes, gates, gu, wd)


def body(queries, new_kv, past_kv, residual, out_weight, norm_gain, routes, gates, w_gate_up, w_down):
    mixed = front(
        queries.reshape(CH, 16, D),
        new_kv.reshape(64, 512),
        past_kv.reshape(64, 512),
        out_weight,
        residual.reshape(16, CH, 16, 256),
    )
    out = experts(
        mixed.reshape(16, 64, 256),
        norm_gain.reshape(1, 256),
        routes.reshape(1024, 8),
        gates.reshape(1024, 8),
        w_gate_up.reshape(256, 2 * FF),
        w_down.reshape(FF, 256),
    )
    return out.reshape(16, 1, 64, 256)


def solution(mesh):
    in_specs = (
        P("ctx", "exp", None, None),
        P("ctx", "exp", None, None),
        P("ctx", "exp", None, None),
        P(None, "exp", None, "ctx"),
        P("exp", "ctx"),
        P("ctx"),
        P(None, "exp", None, None),
        P(None, "exp", None, None),
        P("exp", "ctx", None),
        P("exp", None, "ctx"),
    )
    return jax.shard_map(
        body, mesh=mesh, in_specs=in_specs, out_specs=P(None, "exp", None, "ctx"), check_vma=False
    )
```

```python
import math

import jax
import jax.numpy as jnp
from jax import lax
from jax.experimental import pallas as pl
from jax.experimental.pallas import tpu as pltpu
from jax.sharding import PartitionSpec as P

D = 4096
HEADS = 32
KV_HEADS = 2
HEAD = 128
FF = 1536
HALF = FF // 2
EXT = 128
NY, NX, NZ = 4, 4, 8
CH = 4
NEG = -1e30
SCALE = HEAD ** (-0.5) * math.log2(math.e)
BF = jnp.bfloat16
F32 = jnp.float32
MESH = pl.DeviceIdType.MESH


class Place:
    def __init__(self):
        ctx = lax.axis_index("ctx")
        exp = lax.axis_index("exp")
        self.y = lax.div(ctx, 4)
        self.h = lax.rem(lax.div(ctx, 2), 2)
        self.c = lax.rem(ctx, 2)
        self.x = lax.div(exp, NZ)
        self.z = lax.rem(exp, NZ)
        self.ctx = ctx
        self.exp = exp

    def dev(self, y=None, h=None, c=None, x=None, z=None):
        y = self.y if y is None else y
        h = self.h if h is None else h
        c = self.c if c is None else c
        x = self.x if x is None else x
        z = self.z if z is None else z
        return ((y * 2 + h) * 2 + c, x * NZ + z)


def rem(a, n):
    return lax.rem(a + n, n)


def send(src, dst, ss, rs, dev):
    return pltpu.make_async_remote_copy(
        src_ref=src, dst_ref=dst, send_sem=ss, recv_sem=rs, device_id=dev, device_id_type=MESH
    )


def greet(devs):
    barrier = pltpu.get_barrier_semaphore()
    for dev in devs:
        pl.semaphore_signal(barrier, inc=1, device_id=dev, device_id_type=MESH)


def loop(n, body, start=0):
    lax.fori_loop(start, n, lambda i, _: (body(i), None)[1], None)


def pieces(column, rows):
    lane = lax.broadcasted_iota(jnp.int32, (rows, EXT), 1)
    wide = jnp.broadcast_to(column, (rows, EXT))
    high = wide.astype(BF).astype(F32)
    rest = wide - high
    middle = rest.astype(BF).astype(F32)
    low = rest - middle
    out = jnp.where(lane == 0, high, jnp.where(lane == 1, middle, jnp.where(lane == 2, low, 0.0)))
    return out.astype(BF)


def layer_kernel(
    q_hbm, new_hbm, past_hbm, w_hbm, res_hbm, gain_hbm, routes_hbm, gates_hbm, gu_hbm, wd_hbm, out_ref,
    q_ref, kv, wb, res_ref, gain_ref, routes_ref, gates_ref, gu_ref, wd_ref,
    att, accs, tops, sums, s_ref, psend, precv, mixed, place_ref, place_t, share_ref,
    gains, wgs, picked, disp, arr, sarr, pb, yr, zb, zr, act, eo, rb,
    in_s, kv_s, kv_r, wz_s, wz_r, wx_s, wx_r, at_s, at_r, ah_r, p_s, p_r,
    c_s, c_r, d_s, d_r, a_s, a_r, y_s, y_r, z_s, z_r, az_s, az_r, ay_s, ay_r, ac_s, ac_r, e_s, e_r,
):
    me = Place()
    mate = me.dev(h=1 - me.h)
    sib = me.dev(c=1 - me.c)
    ring = me.h * NZ + me.z

    def ring_dev(step):
        there = rem(ring + step, 2 * NZ)
        return me.dev(h=lax.div(there, NZ), z=lax.rem(there, NZ))

    right, left = ring_dev(1), ring_dev(-1)
    ys = [me.dev(y=rem(me.y + k, NY)) for k in (1, 2, 3)]
    xs = [me.dev(x=rem(me.x + k, NX)) for k in (1, 2, 3)]

    def peer(o):
        x = rem(me.x + lax.div(o, NZ), NX)
        z = rem(me.z + lax.rem(o, NZ), NZ)
        return x * NZ + z

    def peer_dev(e):
        return (me.ctx, e)

    barrier = pltpu.get_barrier_semaphore()
    greet([mate, sib, right, left] + ys)

    def hello(o):
        pl.semaphore_signal(barrier, inc=1, device_id=peer_dev(peer(o)), device_id_type=MESH)

    loop(NX * NZ, hello, 1)

    pairs = [
        (past_hbm, kv.at[0, me.y, me.h, me.c]),
        (new_hbm, kv.at[1, me.y, me.h, me.c]),
        (w_hbm, wb.at[me.h, me.exp]),
        (routes_hbm, routes_ref),
        (gates_hbm, gates_ref),
        (q_hbm, q_ref),
        (gain_hbm, gain_ref),
        (gu_hbm, gu_ref),
        (wd_hbm, wd_ref),
        (res_hbm, res_ref),
    ]
    loads = [pltpu.make_async_copy(src, dst, in_s.at[i]) for i, (src, dst) in enumerate(pairs)]
    for load in loads:
        load.start()

    loads[3].wait()
    loads[4].wait()
    slots = 512
    step = 128
    tri = jnp.where(
        lax.broadcasted_iota(jnp.int32, (step, step), 1) < lax.broadcasted_iota(jnp.int32, (step, step), 0), 1.0, 0.0
    ).astype(BF)
    lane = lax.broadcasted_iota(jnp.int32, (step, 128), 1)
    slot = lax.broadcasted_iota(jnp.int32, (step, slots), 1)
    seen = jnp.zeros((1, 128), F32)

    def by_token(ref, t):
        return jnp.concatenate([ref[2 * t].T, ref[2 * t + 1].T], axis=0)

    for t in range(8):
        half, y = t % 2, t // 2
        routes = by_token(routes_ref, t)
        held = routes < NX * NZ
        target = jnp.sum(jnp.where(held, routes, 0), axis=1, keepdims=True)
        has = jnp.sum(jnp.where(held, 1, 0), axis=1, keepdims=True)
        share_ref[half, y * step : (y + 1) * step] = jnp.sum(
            jnp.where(held, by_token(gates_ref, t), 0.0), axis=1, keepdims=True
        )
        named = jnp.where(has > 0, target, -1)
        part = jnp.where(lane == named, 1.0, 0.0)
        before = jnp.dot(tri, part.astype(BF), preferred_element_type=F32) + seen
        at = jnp.sum(before * part, axis=1, keepdims=True).astype(jnp.int32)
        index = jnp.where(named >= 0, named * 16 + at, -1)
        hot = jnp.where(slot == index, 1.0, 0.0)
        place_ref[half, y * step : (y + 1) * step] = hot.astype(BF)
        place_t[half, :, y * step : (y + 1) * step] = hot.T.astype(BF)
        seen = seen + jnp.sum(part, axis=0, keepdims=True)

    for i in (0, 1, 2):
        loads[i].wait()
    pl.semaphore_wait(barrier, 38)

    def kv_copy(n, y, h, c, out, dev):
        part = kv.at[n, y, h, c]
        return send(part, part, kv_s.at[out], kv_r.at[n, y, h, c], dev)

    kv_copies = []

    def kv_go(n, y, h, c, dev):
        copy = kv_copy(n, y, h, c, len(kv_copies), dev)
        copy.start()
        kv_copies.append(copy)

    def kv_wait(n, y, h, c):
        kv_copy(n, y, h, c, 0, sib).wait_recv()

    for n in range(2):
        kv_go(n, me.y, me.h, me.c, mate)
    for n in range(2):
        for k in (0, 2, 1):
            kv_go(n, me.y, me.h, me.c, ys[k])
        kv_go(n, me.y, me.h, me.c, sib)

    def w_part(shard, x):
        return wb.at[lax.div(shard, NZ), x * NZ + lax.rem(shard, NZ)]

    def w_right(s):
        shard = rem(ring - s + 1, 2 * NZ)
        part = w_part(shard, me.x)
        return send(part, part, wz_s.at[0, s - 1], wz_r.at[shard], right)

    def w_left(s):
        shard = rem(ring + s - 1, 2 * NZ)
        part = w_part(shard, me.x)
        return send(part, part, wz_s.at[1, s - 1], wz_r.at[shard], left)

    def w_wait(shard):
        part = w_part(shard, me.x)
        send(part, part, wz_s.at[0, 0], wz_r.at[shard], right).wait_recv()

    x_up, x_down = xs[0], xs[2]

    def w_x(shard, i):
        if i < 2:
            part = w_part(shard, me.x)
        else:
            part = w_part(shard, rem(me.x + 2 * i - 5, NX)).at[pl.ds((i - 2) * 64, 64)]
        return send(part, part, wx_s.at[i, shard], wx_r.at[i, shard], (x_up, x_down)[i % 2])

    def w_x_wait(shard, i):
        part = w_part(shard, rem(me.x + (-1, 1, 2, 2)[i], NX))
        if i >= 2:
            part = part.at[pl.ds((i - 2) * 64, 64)]
        send(part, part, wx_s.at[i, shard], wx_r.at[i, shard], x_up).wait_recv()

    def w_spread(shard):
        for i in (0, 1):
            w_x(shard, i).start()

    def w_pass(shard):
        for i in (0, 1):
            w_x_wait(shard, i)
            w_x(shard, i + 2).start()

    def ring_send(s):
        w_right(s).start()

        @pl.when(s < NZ)
        def _():
            w_left(s).start()

    def ring_take(s):
        one = rem(ring - s, 2 * NZ)
        w_wait(one)

        @pl.when(s < NZ)
        def _():
            w_wait(rem(ring + s, 2 * NZ))

    def both(s, act_on):
        act_on(rem(ring - s, 2 * NZ))

        @pl.when(s < NZ)
        def _():
            act_on(rem(ring + s, 2 * NZ))

    def ring_step(s):
        ring_take(s)

        @pl.when(s < NZ)
        def _():
            ring_send(s + 1)

        both(s, w_spread)

    ring_send(1)
    w_spread(ring)
    for n in range(2):
        for k in (1, 3, 2):
            y = rem(me.y - k, NY)
            kv_wait(n, y, me.h, me.c)
            kv_go(n, y, me.h, me.c, sib)
    ring_step(1)
    for n in range(2):
        for y in range(NY):
            kv_wait(n, y, me.h, 1 - me.c)
    loads[5].wait()

    mine = me.y * 2 + me.c
    tok = 16
    keys = 512
    per = HEADS // KV_HEADS
    row = lax.broadcasted_iota(jnp.int32, (tok, keys), 0)
    col = lax.broadcasted_iota(jnp.int32, (tok, keys), 1)

    def attend(chunk, half, first):
        spot = lax.div(col, 128) * 256 + half * 128 + lax.rem(col, 128)
        bias = jnp.where(spot <= row + (me.ctx * 64 + chunk * tok), 0.0, NEG)
        for g in range(KV_HEADS):
            q = jnp.concatenate(
                [q_ref[chunk, :, (g * per + i) * HEAD : (g * per + i + 1) * HEAD] for i in range(per)], axis=0
            )
            top = None if first else tops[chunk, g]
            for kt in range(2):
                k = kv[kt, :, half, :, :, g * HEAD : (g + 1) * HEAD].reshape(keys, HEAD)
                s = lax.dot_general(q, k, (((1,), (1,)), ((), ())), preferred_element_type=F32)
                if kt == 1:
                    s = (s.reshape(per, tok, keys) + bias[None]).reshape(per * tok, keys)
                s_ref[:, kt * keys : (kt + 1) * keys] = s
                m = jnp.max(s, axis=1, keepdims=True)
                top = m if top is None else jnp.maximum(top, m)
            total = None
            acc = None
            for kt in range(2):
                p = jnp.exp2((s_ref[:, kt * keys : (kt + 1) * keys] - top) * SCALE)
                v = kv[kt, :, half, :, :, (KV_HEADS + g) * HEAD : (KV_HEADS + g + 1) * HEAD].reshape(keys, HEAD)
                t = jnp.sum(p, axis=1, keepdims=True)
                o = jnp.dot(p.astype(BF), v, preferred_element_type=F32)
                total = t if total is None else total + t
                acc = o if acc is None else acc + o
            if first:
                tops[chunk, g] = top
                sums[chunk, g] = total
                accs[chunk, g] = acc
            else:
                fade = jnp.exp2((tops[chunk, g] - top) * SCALE)
                total = total + sums[chunk, g] * fade
                acc = acc + accs[chunk, g] * fade
                out = (acc / total).astype(BF)
                for i in range(per):
                    att[chunk, mine, :, (g * per + i) * HEAD : (g * per + i + 1) * HEAD] = out[
                        i * tok : (i + 1) * tok
                    ]

    def first_half(chunk):
        attend(chunk, me.h, True)

        @pl.when(lax.rem(chunk, 2) == 1)
        def _():
            ring_step(2 + lax.div(chunk, 2))

    loop(CH, first_half)
    w_pass(ring)

    for n in range(2):
        kv_wait(n, me.y, 1 - me.h, me.c)
        for k in (0, 2, 1):
            kv_go(n, me.y, 1 - me.h, me.c, ys[k])
        kv_go(n, me.y, 1 - me.h, me.c, sib)
    ring_step(4)
    both(1, w_pass)

    loads[6].wait()
    loads[7].wait()
    gains[me.c] = jnp.broadcast_to(gain_ref[...], (8, 256))
    theirs = pl.multiple_of((1 - me.c) * HALF, 128)
    c_copies = [
        send(gu_ref.at[:, pl.ds(theirs, HALF)], wgs.at[:, pl.ds(0, HALF)], c_s.at[0], c_r.at[0], sib),
        send(gu_ref.at[:, pl.ds(theirs + FF, HALF)], wgs.at[:, pl.ds(HALF, HALF)], c_s.at[1], c_r.at[1], sib),
        send(gains.at[me.c], gains.at[me.c], c_s.at[2], c_r.at[2], sib),
    ]
    for n in range(2):
        for k in (1, 3, 2):
            y = rem(me.y - k, NY)
            kv_wait(n, y, 1 - me.h, me.c)
            kv_go(n, y, 1 - me.h, me.c, sib)
    ring_step(5)
    both(2, w_pass)
    for n in range(2):
        for y in range(NY):
            kv_wait(n, y, 1 - me.h, 1 - me.c)
    for copy in c_copies:
        copy.start()

    def who(k):
        return rem(me.y + k, NY) * 2 + me.c

    def att_full(chunk, w, out, dev):
        part = att.at[chunk, w]
        return send(part, part, at_s.at[chunk, out], at_r.at[chunk, w], dev)

    def att_half(chunk, w, part, out, dev):
        cols = att.at[chunk, w, :, pl.ds(part * (D // 2), D // 2)]
        return send(cols, cols, at_s.at[chunk, out], ah_r.at[chunk, part], dev)

    up, down_y = ys[0], ys[2]

    def att_send(chunk, i):
        if i < 3:
            return att_full(chunk, mine, i, (up, down_y, sib)[i])
        if i < 5:
            return att_half(chunk, who((-1, 1)[i - 3]), i - 3, i, (up, down_y)[i - 3])
        return att_full(chunk, who((-1, 1, 2)[i - 5]), i, sib)

    def pass_on(chunk):
        att_full(chunk, who(-1), 0, up).wait_recv()
        att_send(chunk, 3).start()
        att_full(chunk, who(1), 0, up).wait_recv()
        for i in (4, 5, 6):
            att_send(chunk, i).start()

    def pass_last(chunk):
        att_half(chunk, who(2), 0, 0, up).wait_recv()
        att_half(chunk, who(2), 1, 0, up).wait_recv()
        att_send(chunk, 7).start()

    def second_half(chunk):
        attend(chunk, 1 - me.h, False)
        for i in range(3):
            att_send(chunk, i).start()

        @pl.when(chunk < 3)
        def _():
            ring_step(6 + chunk)

        both(chunk + 3, w_pass)

        @pl.when(chunk > 0)
        def _():
            pass_on(chunk - 1)

        @pl.when(chunk > 1)
        def _():
            pass_last(chunk - 2)

    loop(CH, second_half)
    pass_on(CH - 1)
    pass_last(CH - 2)

    def w_arrive(half):
        def one(z):
            shard = half * NZ + z
            for i in (2, 3):
                w_x_wait(shard, i)

        loop(NZ, one)

    both(NZ - 1, w_pass)
    w_pass(rem(ring - NZ, 2 * NZ))
    w_arrive(1 - me.h)

    def p_copy(chunk):
        return send(psend.at[chunk], precv.at[chunk], p_s.at[chunk], p_r.at[chunk], mate)

    def rows_of(chunk):
        return att[chunk].reshape(8 * tok, D)

    def for_mate(chunk):
        for y in range(NY):
            att_full(chunk, y * 2 + 1 - me.c, 0, sib).wait_recv()
        psend[chunk] = jnp.dot(rows_of(chunk), wb[1 - me.h].reshape(D, 256), preferred_element_type=F32).astype(BF)
        p_copy(chunk).start()

    loop(CH - 1, for_mate)
    pass_last(CH - 1)
    loop(CH, for_mate, CH - 1)
    w_arrive(me.h)
    loads[9].wait()

    def put(chunk, half, value):
        for j in range(8):
            y, c = j // 2, j % 2
            mixed[half, y, c, chunk] = res_ref[y, half, c, chunk].astype(F32) + value[j * tok : (j + 1) * tok].astype(
                F32
            )

    def for_me(chunk):
        put(chunk, me.h, jnp.dot(rows_of(chunk), wb[me.h].reshape(D, 256), preferred_element_type=F32))

    loop(CH, for_me)

    def pick(half):
        rows = (mixed[half].reshape(512, 256) * gain_ref[...]).astype(BF)
        return jnp.dot(place_t[half], rows, preferred_element_type=F32)

    picked[...] = pick(me.h)

    def from_mate(chunk):
        p_copy(chunk).wait_recv()
        put(chunk, 1 - me.h, precv[chunk])

    loop(CH, from_mate)
    disp[...] = (picked[...] + pick(1 - me.h)).astype(BF).reshape(32, 16, 256)

    def d_copy(o):
        e = peer(o)
        return send(disp.at[e], arr.at[me.exp], d_s.at[o], d_r.at[me.exp], peer_dev(e))

    loop(NX * NZ, lambda o: d_copy(o).start(), 1)
    arr[me.exp] = disp[me.exp]
    def src_x(q):
        return rem(me.x - q, NX)

    def a_copy(q):
        x = src_x(q)
        part = arr.at[pl.ds(x * NZ, NZ)]
        return send(part, sarr.at[pl.ds(x * NZ, NZ)], a_s.at[x], a_r.at[x], sib)

    def collect(q):
        x = src_x(q)

        def one(z):
            e = x * NZ + z

            @pl.when(e != me.exp)
            def _():
                send(disp.at[0], arr.at[e], d_s.at[0], d_r.at[e], sib).wait_recv()

        loop(NZ, one)
        a_copy(q).start()

    for q in range(CH):
        collect(q)
    loads[8].wait()
    c_copies[0].wait_recv()
    c_copies[1].wait_recv()
    send(gains.at[me.c], gains.at[1 - me.c], c_s.at[2], c_r.at[2], sib).wait_recv()
    ours = pl.multiple_of(me.c * HALF, 128)

    def y_copy(q, k):
        there = rem(me.y + k, NY)
        part = pb.at[q, pl.ds(there * 32, 32)]
        return send(part, yr.at[q, k - 1], y_s.at[q, k - 1], y_r.at[q, k - 1], ys[k - 1])

    def gate_up(q):
        x = src_x(q)
        a_copy(q).wait_recv()
        mine = arr[pl.ds(x * NZ, NZ)].reshape(128, 256)
        other = sarr[pl.ds(x * NZ, NZ)].reshape(128, 256)
        a = mine.astype(F32) / gains[me.c, 0:1]
        b = other.astype(F32) / gains[1 - me.c, 0:1]
        squares = jnp.sum(a * a, axis=1, keepdims=True) + jnp.sum(b * b, axis=1, keepdims=True)
        pb[q, :, FF * 1 :] = pieces(squares, 128)
        gate = jnp.dot(mine, gu_ref[:, pl.ds(ours, HALF)], preferred_element_type=F32)
        gate += jnp.dot(other, wgs[:, 0:HALF], preferred_element_type=F32)
        pb[q, :, 0:HALF] = gate.astype(BF)
        up = jnp.dot(mine, gu_ref[:, pl.ds(ours + FF, HALF)], preferred_element_type=F32)
        up += jnp.dot(other, wgs[:, HALF:FF], preferred_element_type=F32)
        pb[q, :, HALF:FF] = up.astype(BF)

    def y_send(q):
        for k in (1, 3, 2):
            y_copy(q, k).start()

    def z_copy(q):
        part = zb.at[q, pl.ds((1 - me.h) * 16, 16)]
        return send(part, zr.at[q], z_s.at[q], z_r.at[q], mate)

    def y_sum(q):
        total = pb[q, pl.ds(pl.multiple_of(me.y * 32, 32), 32)].astype(F32)
        for k in (1, 2, 3):
            y_copy(q, k).wait_recv()
            total = total + yr[q, k - 1].astype(F32)
        zb[q, :, 0:FF] = total[:, 0:FF].astype(BF)
        zb[q, :, FF:] = pieces(jnp.sum(total[:, FF:], axis=1, keepdims=True), 32)
        z_copy(q).start()


    def az_copy(q):
        part = act.at[q, me.c, me.y, me.h]
        return send(part, part, az_s.at[q], az_r.at[q], mate)

    def activate(q):
        z_copy(q).wait_recv()
        total = zb[q, pl.ds(pl.multiple_of(me.h * 16, 16), 16)].astype(F32) + zr[q].astype(F32)
        squares = jnp.sum(total[:, FF:], axis=1, keepdims=True)
        scale = lax.rsqrt(squares / D + 1e-6)
        gate = total[:, 0:HALF] * scale
        up = total[:, HALF:FF] * scale
        act[q, me.c, me.y, me.h] = (gate / (1.0 + jnp.exp(-gate)) * up).astype(BF)
        az_copy(q).start()


    def ay_copy(q, y, k):
        part = act.at[q, me.c, y]
        return send(part, part, ay_s.at[q, k - 1], ay_r.at[q, y], ys[k - 1])

    def spread(q):
        part = act.at[q, me.c, me.y, 1 - me.h]
        send(part, part, az_s.at[q], az_r.at[q], mate).wait_recv()
        for k in (1, 2, 3):
            ay_copy(q, me.y, k).start()


    def ac_copy(q, c):
        part = act.at[q, c]
        return send(part, part, ac_s.at[q], ac_r.at[q], sib)

    def share(q):
        for k in (1, 2, 3):
            ay_copy(q, rem(me.y - k, NY), k).wait_recv()
        ac_copy(q, me.c).start()


    def e_copy(o):
        e = peer(o)
        return send(eo.at[e], rb.at[me.exp], e_s.at[o], e_r.at[me.exp], peer_dev(e))

    def down(q):
        x = src_x(q)
        ac_copy(q, 1 - me.c).wait_recv()
        value = jnp.dot(act[q, 0].reshape(128, HALF), wd_ref[0:HALF], preferred_element_type=F32)
        value += jnp.dot(act[q, 1].reshape(128, HALF), wd_ref[HALF:FF], preferred_element_type=F32)
        eo[pl.ds(x * NZ, NZ)] = value.astype(BF).reshape(NZ, 16, 256)

        def back(z):
            e_copy((NX - q) % NX * NZ + z).start()

        loop(NZ, back, 1 if q == 0 else 0)

    gate_up(0)
    y_send(0)
    gate_up(1)
    y_send(1)
    gate_up(2)
    gate_up(3)
    y_sum(0)
    y_send(2)
    y_sum(1)
    y_send(3)
    y_sum(2)
    activate(0)
    y_sum(3)
    activate(1)
    activate(2)
    spread(0)
    activate(3)
    spread(1)
    share(0)
    spread(2)
    share(1)
    down(0)
    spread(3)
    share(2)
    down(1)
    share(3)
    down(2)
    down(3)
    rb[me.exp] = eo[me.exp]

    def home(e):
        @pl.when(e != me.exp)
        def _():
            send(eo.at[0], rb.at[e], e_s.at[0], e_r.at[e], sib).wait_recv()

    loop(NX * NZ, home)
    back = rb[...].reshape(slots, 256)
    for half in range(2):
        got = jnp.dot(place_ref[half], back, preferred_element_type=F32)
        value = mixed[half].reshape(512, 256) + share_ref[half] * got
        out_ref[:, half] = value.astype(BF).reshape(NY, 128, 256)

    for copy in c_copies + kv_copies:
        copy.wait_send()

    def ring_left(s):
        w_right(s).wait_send()

        @pl.when(s < NZ)
        def _():
            w_left(s).wait_send()

    loop(NZ + 1, ring_left, 1)

    def x_left(shard):
        for i in range(4):
            w_x(shard, i).wait_send()

    loop(2 * NZ, x_left)

    def peers_left(o):
        d_copy(o).wait_send()
        e_copy(o).wait_send()

    loop(NX * NZ, peers_left, 1)

    def chunk_left(q):
        for i in range(8):
            att_send(q, i).wait_send()
        p_copy(q).wait_send()
        a_copy(q).wait_send()
        z_copy(q).wait_send()
        az_copy(q).wait_send()
        ac_copy(q, me.c).wait_send()
        for k in (1, 2, 3):
            y_copy(q, k).wait_send()
            ay_copy(q, me.y, k).wait_send()

    loop(CH, chunk_left)


def body(queries, new_kv, past_kv, residual, out_weight, norm_gain, routes, gates, w_gate_up, w_down):
    sem = pltpu.SemaphoreType.DMA
    wide = FF + EXT
    out = pl.pallas_call(
        layer_kernel,
        out_shape=jax.ShapeDtypeStruct((NY, 2, 128, 256), BF),
        in_specs=[pl.BlockSpec(memory_space=pl.ANY)] * 10,
        out_specs=pl.BlockSpec(memory_space=pltpu.VMEM),
        scratch_shapes=[
            pltpu.VMEM((CH, 16, D), BF),
            pltpu.VMEM((2, NY, 2, 2, 64, 512), BF),
            pltpu.VMEM((2, 32, 128, 256), BF),
            pltpu.VMEM((NY, 2, 2, CH, 16, 256), BF),
            pltpu.VMEM((1, 256), F32),
            pltpu.VMEM((16, 8, 64), jnp.int32),
            pltpu.VMEM((16, 8, 64), F32),
            pltpu.VMEM((256, 2 * FF), BF),
            pltpu.VMEM((FF, 256), BF),
            pltpu.VMEM((CH, 8, 16, D), BF),
            pltpu.VMEM((CH, KV_HEADS, 256, HEAD), F32),
            pltpu.VMEM((CH, KV_HEADS, 256, 1), F32),
            pltpu.VMEM((CH, KV_HEADS, 256, 1), F32),
            pltpu.VMEM((256, 1024), F32),
            pltpu.VMEM((CH, 128, 256), BF),
            pltpu.VMEM((CH, 128, 256), BF),
            pltpu.VMEM((2, NY, 2, CH, 16, 256), F32),
            pltpu.VMEM((2, 512, 512), BF),
            pltpu.VMEM((2, 512, 512), BF),
            pltpu.VMEM((2, 512, 1), F32),
            pltpu.VMEM((2, 8, 256), F32),
            pltpu.VMEM((256, FF), BF),
            pltpu.VMEM((512, 256), F32),
            pltpu.VMEM((32, 16, 256), BF),
            pltpu.VMEM((32, 16, 256), BF),
            pltpu.VMEM((32, 16, 256), BF),
            pltpu.VMEM((CH, 128, wide), BF),
            pltpu.VMEM((CH, 3, 32, wide), BF),
            pltpu.VMEM((CH, 32, wide), BF),
            pltpu.VMEM((CH, 16, wide), BF),
            pltpu.VMEM((CH, 2, NY, 2, 16, HALF), BF),
            pltpu.VMEM((32, 16, 256), BF),
            pltpu.VMEM((32, 16, 256), BF),
            sem((10,)),
            sem((30,)), sem((2, NY, 2, 2)),
            sem((2, 8)), sem((16,)),
            sem((4, 16)), sem((4, 16)),
            sem((CH, 8)), sem((CH, 8)), sem((CH, 2)),
            sem((CH,)), sem((CH,)),
            sem((3,)), sem((3,)),
            sem((32,)), sem((32,)),
            sem((4,)), sem((4,)),
            sem((CH, 3)), sem((CH, 3)),
            sem((CH,)), sem((CH,)),
            sem((CH,)), sem((CH,)),
            sem((CH, 3)), sem((CH, NY)),
            sem((CH,)), sem((CH,)),
            sem((32,)), sem((32,)),
        ],
        compiler_params=pltpu.CompilerParams(
            collective_id=0, has_side_effects=True, vmem_limit_bytes=56 * 2**20
        ),
        name="layer",
    )(
        queries.reshape(CH, 16, D),
        new_kv.reshape(64, 512),
        past_kv.reshape(64, 512),
        out_weight,
        residual.reshape(NY, 2, 2, CH, 16, 256),
        norm_gain.reshape(1, 256),
        jnp.swapaxes(routes.reshape(16, 64, 8), 1, 2),
        jnp.swapaxes(gates.reshape(16, 64, 8), 1, 2),
        w_gate_up.reshape(256, 2 * FF),
        w_down.reshape(FF, 256),
    )
    return out.reshape(16, 1, 64, 256)


def solution(mesh):
    in_specs = (
        P("ctx", "exp", None, None),
        P("ctx", "exp", None, None),
        P("ctx", "exp", None, None),
        P(None, "exp", None, "ctx"),
        P("exp", "ctx"),
        P("ctx"),
        P(None, "exp", None, None),
        P(None, "exp", None, None),
        P("exp", "ctx", None),
        P("exp", None, "ctx"),
    )
    return jax.shard_map(
        body, mesh=mesh, in_specs=in_specs, out_specs=P(None, "exp", None, "ctx"), check_vma=False
    )
```

```python
import math

import jax
import jax.numpy as jnp
from jax import lax
from jax.experimental import pallas as pl
from jax.experimental.pallas import tpu as pltpu
from jax.sharding import PartitionSpec as P

D = 4096
HEADS = 32
KV_HEADS = 2
HEAD = 128
FF = 1536
HALF = FF // 2
EXT = 128
NY, NX, NZ = 4, 4, 8
CH = 4
NEG = -1e30
SCALE = HEAD ** (-0.5) * math.log2(math.e)
BF = jnp.bfloat16
F32 = jnp.float32
MESH = pl.DeviceIdType.MESH


class Place:
    def __init__(self):
        ctx = lax.axis_index("ctx")
        exp = lax.axis_index("exp")
        self.y = lax.div(ctx, 4)
        self.h = lax.rem(lax.div(ctx, 2), 2)
        self.c = lax.rem(ctx, 2)
        self.x = lax.div(exp, NZ)
        self.z = lax.rem(exp, NZ)
        self.ctx = ctx
        self.exp = exp

    def dev(self, y=None, h=None, c=None, x=None, z=None):
        y = self.y if y is None else y
        h = self.h if h is None else h
        c = self.c if c is None else c
        x = self.x if x is None else x
        z = self.z if z is None else z
        return ((y * 2 + h) * 2 + c, x * NZ + z)


def rem(a, n):
    return lax.rem(a + n, n)


def send(src, dst, ss, rs, dev):
    return pltpu.make_async_remote_copy(
        src_ref=src, dst_ref=dst, send_sem=ss, recv_sem=rs, device_id=dev, device_id_type=MESH
    )


def greet(devs):
    barrier = pltpu.get_barrier_semaphore()
    for dev in devs:
        pl.semaphore_signal(barrier, inc=1, device_id=dev, device_id_type=MESH)


def loop(n, body, start=0):
    lax.fori_loop(start, n, lambda i, _: (body(i), None)[1], None)


def pieces(column, rows):
    lane = lax.broadcasted_iota(jnp.int32, (rows, EXT), 1)
    wide = jnp.broadcast_to(column, (rows, EXT))
    high = wide.astype(BF).astype(F32)
    rest = wide - high
    middle = rest.astype(BF).astype(F32)
    low = rest - middle
    out = jnp.where(lane == 0, high, jnp.where(lane == 1, middle, jnp.where(lane == 2, low, 0.0)))
    return out.astype(BF)


def layer_kernel(
    q_hbm, new_hbm, past_hbm, w_hbm, res_hbm, gain_hbm, routes_hbm, gates_hbm, gu_hbm, wd_hbm, out_ref,
    q_ref, kv, wb, res_ref, gain_ref, routes_ref, gates_ref, gu_ref, wd_ref,
    att, accs, tops, sums, s_ref, psend, precv, mixed, place_ref, place_t, share_ref,
    gains, wgs, picked, disp, arr, sarr, pb, yr, zb, zr, act, eo, rb,
    in_s, kv_s, kv_r, wz_s, wz_r, wx_s, wx_r, at_s, at_r, ah_r, p_s, p_r,
    c_s, c_r, d_s, d_r, a_s, a_r, y_s, y_r, z_s, z_r, az_s, az_r, ay_s, ay_r, ac_s, ac_r, e_s, e_r,
):
    me = Place()
    mate = me.dev(h=1 - me.h)
    sib = me.dev(c=1 - me.c)
    ring = me.h * NZ + me.z

    def ring_dev(step):
        there = rem(ring + step, 2 * NZ)
        return me.dev(h=lax.div(there, NZ), z=lax.rem(there, NZ))

    right, left = ring_dev(1), ring_dev(-1)
    ys = [me.dev(y=rem(me.y + k, NY)) for k in (1, 2, 3)]
    xs = [me.dev(x=rem(me.x + k, NX)) for k in (1, 2, 3)]

    def peer(o):
        x = rem(me.x + lax.div(o, NZ), NX)
        z = rem(me.z + lax.rem(o, NZ), NZ)
        return x * NZ + z

    def peer_dev(e):
        return (me.ctx, e)

    barrier = pltpu.get_barrier_semaphore()
    greet([mate, sib, right, left] + ys)

    def hello(o):
        pl.semaphore_signal(barrier, inc=1, device_id=peer_dev(peer(o)), device_id_type=MESH)

    loop(NX * NZ, hello, 1)

    pairs = [
        (past_hbm, kv.at[0, me.y, me.h, me.c]),
        (new_hbm, kv.at[1, me.y, me.h, me.c]),
        (w_hbm, wb.at[me.h, me.exp]),
        (routes_hbm, routes_ref),
        (gates_hbm, gates_ref),
        (q_hbm, q_ref),
        (gain_hbm, gain_ref),
        (gu_hbm, gu_ref),
        (wd_hbm, wd_ref),
        (res_hbm, res_ref),
    ]
    loads = [pltpu.make_async_copy(src, dst, in_s.at[i]) for i, (src, dst) in enumerate(pairs)]
    for load in loads:
        load.start()

    loads[3].wait()
    loads[4].wait()
    slots = 512
    step = 128
    tri = jnp.where(
        lax.broadcasted_iota(jnp.int32, (step, step), 1) < lax.broadcasted_iota(jnp.int32, (step, step), 0), 1.0, 0.0
    ).astype(BF)
    lane = lax.broadcasted_iota(jnp.int32, (step, 128), 1)
    slot = lax.broadcasted_iota(jnp.int32, (step, slots), 1)
    seen = jnp.zeros((1, 128), F32)

    def by_token(ref, t):
        return jnp.concatenate([ref[2 * t].T, ref[2 * t + 1].T], axis=0)

    for t in range(8):
        half, y = t % 2, t // 2
        routes = by_token(routes_ref, t)
        held = routes < NX * NZ
        target = jnp.sum(jnp.where(held, routes, 0), axis=1, keepdims=True)
        has = jnp.sum(jnp.where(held, 1, 0), axis=1, keepdims=True)
        share_ref[half, y * step : (y + 1) * step] = jnp.sum(
            jnp.where(held, by_token(gates_ref, t), 0.0), axis=1, keepdims=True
        )
        named = jnp.where(has > 0, target, -1)
        part = jnp.where(lane == named, 1.0, 0.0)
        before = jnp.dot(tri, part.astype(BF), preferred_element_type=F32) + seen
        at = jnp.sum(before * part, axis=1, keepdims=True).astype(jnp.int32)
        index = jnp.where(named >= 0, named * 16 + at, -1)
        hot = jnp.where(slot == index, 1.0, 0.0)
        place_ref[half, y * step : (y + 1) * step] = hot.astype(BF)
        place_t[half, :, y * step : (y + 1) * step] = hot.T.astype(BF)
        seen = seen + jnp.sum(part, axis=0, keepdims=True)

    for i in (0, 1, 2):
        loads[i].wait()
    pl.semaphore_wait(barrier, 38)

    def kv_copy(n, y, h, c, out, dev):
        part = kv.at[n, y, h, c]
        return send(part, part, kv_s.at[out], kv_r.at[n, y, h, c], dev)

    kv_copies = []

    def kv_go(n, y, h, c, dev):
        copy = kv_copy(n, y, h, c, len(kv_copies), dev)
        copy.start()
        kv_copies.append(copy)

    def kv_wait(n, y, h, c):
        kv_copy(n, y, h, c, 0, sib).wait_recv()

    for n in range(2):
        kv_go(n, me.y, me.h, me.c, mate)
    for n in range(2):
        for k in (0, 2, 1):
            kv_go(n, me.y, me.h, me.c, ys[k])
        kv_go(n, me.y, me.h, me.c, sib)

    def w_part(shard, x):
        return wb.at[lax.div(shard, NZ), x * NZ + lax.rem(shard, NZ)]

    def w_right(s):
        shard = rem(ring - s + 1, 2 * NZ)
        part = w_part(shard, me.x)
        return send(part, part, wz_s.at[0, s - 1], wz_r.at[shard], right)

    def w_left(s):
        shard = rem(ring + s - 1, 2 * NZ)
        part = w_part(shard, me.x)
        return send(part, part, wz_s.at[1, s - 1], wz_r.at[shard], left)

    def w_wait(shard):
        part = w_part(shard, me.x)
        send(part, part, wz_s.at[0, 0], wz_r.at[shard], right).wait_recv()

    x_up, x_down = xs[0], xs[2]

    def w_x(shard, i):
        if i < 2:
            part = w_part(shard, me.x)
        else:
            part = w_part(shard, rem(me.x + 2 * i - 5, NX)).at[pl.ds((i - 2) * 64, 64)]
        return send(part, part, wx_s.at[i, shard], wx_r.at[i, shard], (x_up, x_down)[i % 2])

    def w_x_wait(shard, i):
        part = w_part(shard, rem(me.x + (-1, 1, 2, 2)[i], NX))
        if i >= 2:
            part = part.at[pl.ds((i - 2) * 64, 64)]
        send(part, part, wx_s.at[i, shard], wx_r.at[i, shard], x_up).wait_recv()

    def w_spread(shard):
        for i in (0, 1):
            w_x(shard, i).start()

    def w_pass(shard):
        for i in (0, 1):
            w_x_wait(shard, i)
            w_x(shard, i + 2).start()

    def ring_send(s):
        w_right(s).start()

        @pl.when(s < NZ)
        def _():
            w_left(s).start()

    def ring_take(s):
        one = rem(ring - s, 2 * NZ)
        w_wait(one)

        @pl.when(s < NZ)
        def _():
            w_wait(rem(ring + s, 2 * NZ))

    def both(s, act_on):
        act_on(rem(ring - s, 2 * NZ))

        @pl.when(s < NZ)
        def _():
            act_on(rem(ring + s, 2 * NZ))

    def ring_step(s):
        ring_take(s)

        @pl.when(s < NZ)
        def _():
            ring_send(s + 1)

        both(s, w_spread)

    ring_send(1)
    w_spread(ring)
    for n in range(2):
        for k in (1, 3, 2):
            y = rem(me.y - k, NY)
            kv_wait(n, y, me.h, me.c)
            kv_go(n, y, me.h, me.c, sib)
    ring_step(1)
    for n in range(2):
        for y in range(NY):
            kv_wait(n, y, me.h, 1 - me.c)
    loads[5].wait()

    mine = me.y * 2 + me.c
    tok = 16
    keys = 512
    per = HEADS // KV_HEADS
    row = lax.broadcasted_iota(jnp.int32, (tok, keys), 0)
    col = lax.broadcasted_iota(jnp.int32, (tok, keys), 1)

    def attend(chunk, half, first):
        spot = lax.div(col, 128) * 256 + half * 128 + lax.rem(col, 128)
        bias = jnp.where(spot <= row + (me.ctx * 64 + chunk * tok), 0.0, NEG)
        for g in range(KV_HEADS):
            q = jnp.concatenate(
                [q_ref[chunk, :, (g * per + i) * HEAD : (g * per + i + 1) * HEAD] for i in range(per)], axis=0
            )
            top = None if first else tops[chunk, g]
            for kt in range(2):
                k = kv[kt, :, half, :, :, g * HEAD : (g + 1) * HEAD].reshape(keys, HEAD)
                s = lax.dot_general(q, k, (((1,), (1,)), ((), ())), preferred_element_type=F32)
                if kt == 1:
                    s = (s.reshape(per, tok, keys) + bias[None]).reshape(per * tok, keys)
                s_ref[:, kt * keys : (kt + 1) * keys] = s
                m = jnp.max(s, axis=1, keepdims=True)
                top = m if top is None else jnp.maximum(top, m)
            total = None
            acc = None
            for kt in range(2):
                p = jnp.exp2((s_ref[:, kt * keys : (kt + 1) * keys] - top) * SCALE)
                v = kv[kt, :, half, :, :, (KV_HEADS + g) * HEAD : (KV_HEADS + g + 1) * HEAD].reshape(keys, HEAD)
                t = jnp.sum(p, axis=1, keepdims=True)
                o = jnp.dot(p.astype(BF), v, preferred_element_type=F32)
                total = t if total is None else total + t
                acc = o if acc is None else acc + o
            if first:
                tops[chunk, g] = top
                sums[chunk, g] = total
                accs[chunk, g] = acc
            else:
                fade = jnp.exp2((tops[chunk, g] - top) * SCALE)
                total = total + sums[chunk, g] * fade
                acc = acc + accs[chunk, g] * fade
                out = (acc / total).astype(BF)
                for i in range(per):
                    att[chunk, mine, :, (g * per + i) * HEAD : (g * per + i + 1) * HEAD] = out[
                        i * tok : (i + 1) * tok
                    ]

    def first_half(chunk):
        attend(chunk, me.h, True)

        @pl.when(lax.rem(chunk, 2) == 1)
        def _():
            ring_step(2 + lax.div(chunk, 2))

    loop(CH, first_half)
    w_pass(ring)

    for n in range(2):
        kv_wait(n, me.y, 1 - me.h, me.c)
        for k in (0, 2, 1):
            kv_go(n, me.y, 1 - me.h, me.c, ys[k])
        kv_go(n, me.y, 1 - me.h, me.c, sib)
    ring_step(4)
    both(1, w_pass)

    loads[6].wait()
    loads[7].wait()
    gains[me.c] = jnp.broadcast_to(gain_ref[...], (8, 256))
    theirs = pl.multiple_of((1 - me.c) * HALF, 128)
    c_copies = [
        send(gu_ref.at[:, pl.ds(theirs, HALF)], wgs.at[:, pl.ds(0, HALF)], c_s.at[0], c_r.at[0], sib),
        send(gu_ref.at[:, pl.ds(theirs + FF, HALF)], wgs.at[:, pl.ds(HALF, HALF)], c_s.at[1], c_r.at[1], sib),
        send(gains.at[me.c], gains.at[me.c], c_s.at[2], c_r.at[2], sib),
    ]
    for n in range(2):
        for k in (1, 3, 2):
            y = rem(me.y - k, NY)
            kv_wait(n, y, 1 - me.h, me.c)
            kv_go(n, y, 1 - me.h, me.c, sib)
    ring_step(5)
    both(2, w_pass)
    for n in range(2):
        for y in range(NY):
            kv_wait(n, y, 1 - me.h, 1 - me.c)
    for copy in c_copies:
        copy.start()

    def who(k):
        return rem(me.y + k, NY) * 2 + me.c

    def att_full(chunk, w, out, dev):
        part = att.at[chunk, w]
        return send(part, part, at_s.at[chunk, out], at_r.at[chunk, w], dev)

    def att_half(chunk, w, part, out, dev):
        cols = att.at[chunk, w, :, pl.ds(part * (D // 2), D // 2)]
        return send(cols, cols, at_s.at[chunk, out], ah_r.at[chunk, part], dev)

    up, down_y = ys[0], ys[2]

    def att_send(chunk, i):
        if i < 3:
            return att_full(chunk, mine, i, (up, down_y, sib)[i])
        if i < 5:
            return att_half(chunk, who((-1, 1)[i - 3]), i - 3, i, (up, down_y)[i - 3])
        return att_full(chunk, who((-1, 1, 2)[i - 5]), i, sib)

    def pass_on(chunk):
        att_full(chunk, who(-1), 0, up).wait_recv()
        att_send(chunk, 3).start()
        att_full(chunk, who(1), 0, up).wait_recv()
        for i in (4, 5, 6):
            att_send(chunk, i).start()

    def pass_last(chunk):
        att_half(chunk, who(2), 0, 0, up).wait_recv()
        att_half(chunk, who(2), 1, 0, up).wait_recv()
        att_send(chunk, 7).start()

    def second_half(chunk):
        attend(chunk, 1 - me.h, False)
        for i in range(3):
            att_send(chunk, i).start()

        @pl.when(chunk < 3)
        def _():
            ring_step(6 + chunk)

        both(chunk + 3, w_pass)

        @pl.when(chunk > 0)
        def _():
            pass_on(chunk - 1)

        @pl.when(chunk > 1)
        def _():
            pass_last(chunk - 2)

    loop(CH, second_half)
    pass_on(CH - 1)
    pass_last(CH - 2)

    def w_arrive(half):
        def one(z):
            shard = half * NZ + z
            for i in (2, 3):
                w_x_wait(shard, i)

        loop(NZ, one)

    both(NZ - 1, w_pass)
    w_pass(rem(ring - NZ, 2 * NZ))
    w_arrive(1 - me.h)

    def p_copy(chunk):
        return send(psend.at[chunk], precv.at[chunk], p_s.at[chunk], p_r.at[chunk], mate)

    def rows_of(chunk):
        return att[chunk].reshape(8 * tok, D)

    def for_mate(chunk):
        for y in range(NY):
            att_full(chunk, y * 2 + 1 - me.c, 0, sib).wait_recv()
        psend[chunk] = jnp.dot(rows_of(chunk), wb[1 - me.h].reshape(D, 256), preferred_element_type=F32).astype(BF)
        p_copy(chunk).start()

    loop(CH - 1, for_mate)
    pass_last(CH - 1)
    loop(CH, for_mate, CH - 1)
    w_arrive(me.h)
    loads[9].wait()

    def put(chunk, half, value):
        for j in range(8):
            y, c = j // 2, j % 2
            mixed[half, y, c, chunk] = res_ref[y, half, c, chunk].astype(F32) + value[j * tok : (j + 1) * tok].astype(
                F32
            )

    def for_me(chunk):
        put(chunk, me.h, jnp.dot(rows_of(chunk), wb[me.h].reshape(D, 256), preferred_element_type=F32))

    loop(CH, for_me)

    def pick(half):
        rows = (mixed[half].reshape(512, 256) * gain_ref[...]).astype(BF)
        return jnp.dot(place_t[half], rows, preferred_element_type=F32)

    picked[...] = pick(me.h)

    def from_mate(chunk):
        p_copy(chunk).wait_recv()
        put(chunk, 1 - me.h, precv[chunk])

    loop(CH, from_mate)
    disp[...] = (picked[...] + pick(1 - me.h)).astype(BF).reshape(32, 16, 256)

    def d_copy(o):
        e = peer(o)
        return send(disp.at[e], arr.at[me.exp], d_s.at[o], d_r.at[me.exp], peer_dev(e))

    def d_start(o):
        d_copy(o).start()

    def d_left(o):
        d_copy(o).wait_send()

    loop(2 * NZ, d_start, 1)
    arr[me.exp] = disp[me.exp]
    loop(NZ, d_left, 1)
    loop(3 * NZ, d_start, 2 * NZ)
    loop(2 * NZ, d_left, NZ)
    loop(4 * NZ, d_start, 3 * NZ)
    def src_x(q):
        return rem(me.x - q, NX)

    def a_copy(q):
        x = src_x(q)
        part = arr.at[pl.ds(x * NZ, NZ)]
        return send(part, sarr.at[pl.ds(x * NZ, NZ)], a_s.at[x], a_r.at[x], sib)

    def collect(q):
        x = src_x(q)

        def one(z):
            e = x * NZ + z

            @pl.when(e != me.exp)
            def _():
                send(disp.at[0], arr.at[e], d_s.at[0], d_r.at[e], sib).wait_recv()

        loop(NZ, one)
        a_copy(q).start()

    for copy in c_copies + kv_copies:
        copy.wait_send()

    def ring_left(s):
        w_right(s).wait_send()

        @pl.when(s < NZ)
        def _():
            w_left(s).wait_send()

    loop(NZ + 1, ring_left, 1)

    def x_left(shard):
        for i in range(4):
            w_x(shard, i).wait_send()

    loop(2 * NZ, x_left)

    def att_left(q):
        for i in range(8):
            att_send(q, i).wait_send()
        p_copy(q).wait_send()

    loop(CH, att_left)
    collect(0)
    loads[8].wait()
    c_copies[0].wait_recv()
    c_copies[1].wait_recv()
    send(gains.at[me.c], gains.at[1 - me.c], c_s.at[2], c_r.at[2], sib).wait_recv()
    ours = pl.multiple_of(me.c * HALF, 128)

    def y_copy(q, k):
        there = rem(me.y + k, NY)
        part = pb.at[q, pl.ds(there * 32, 32)]
        return send(part, yr.at[q, k - 1], y_s.at[q, k - 1], y_r.at[q, k - 1], ys[k - 1])

    def gate_up(q):
        x = src_x(q)
        a_copy(q).wait_recv()
        mine = arr[pl.ds(x * NZ, NZ)].reshape(128, 256)
        other = sarr[pl.ds(x * NZ, NZ)].reshape(128, 256)
        a = mine.astype(F32) / gains[me.c, 0:1]
        b = other.astype(F32) / gains[1 - me.c, 0:1]
        squares = jnp.sum(a * a, axis=1, keepdims=True) + jnp.sum(b * b, axis=1, keepdims=True)
        pb[q, :, FF * 1 :] = pieces(squares, 128)
        gate = jnp.dot(mine, gu_ref[:, pl.ds(ours, HALF)], preferred_element_type=F32)
        gate += jnp.dot(other, wgs[:, 0:HALF], preferred_element_type=F32)
        pb[q, :, 0:HALF] = gate.astype(BF)
        up = jnp.dot(mine, gu_ref[:, pl.ds(ours + FF, HALF)], preferred_element_type=F32)
        up += jnp.dot(other, wgs[:, HALF:FF], preferred_element_type=F32)
        pb[q, :, HALF:FF] = up.astype(BF)

    def y_send(q):
        for k in (1, 3, 2):
            y_copy(q, k).start()

    def z_copy(q):
        part = zb.at[q, pl.ds((1 - me.h) * 16, 16)]
        return send(part, zr.at[q], z_s.at[q], z_r.at[q], mate)

    def y_sum(q):
        total = pb[q, pl.ds(pl.multiple_of(me.y * 32, 32), 32)].astype(F32)
        for k in (1, 2, 3):
            y_copy(q, k).wait_recv()
            total = total + yr[q, k - 1].astype(F32)
        zb[q, :, 0:FF] = total[:, 0:FF].astype(BF)
        zb[q, :, FF:] = pieces(jnp.sum(total[:, FF:], axis=1, keepdims=True), 32)
        z_copy(q).start()


    def az_copy(q):
        part = act.at[q, me.c, me.y, me.h]
        return send(part, part, az_s.at[q], az_r.at[q], mate)

    def activate(q):
        z_copy(q).wait_recv()
        total = zb[q, pl.ds(pl.multiple_of(me.h * 16, 16), 16)].astype(F32) + zr[q].astype(F32)
        squares = jnp.sum(total[:, FF:], axis=1, keepdims=True)
        scale = lax.rsqrt(squares / D + 1e-6)
        gate = total[:, 0:HALF] * scale
        up = total[:, HALF:FF] * scale
        act[q, me.c, me.y, me.h] = (gate / (1.0 + jnp.exp(-gate)) * up).astype(BF)
        az_copy(q).start()


    def ay_copy(q, y, k):
        part = act.at[q, me.c, y]
        return send(part, part, ay_s.at[q, k - 1], ay_r.at[q, y], ys[k - 1])

    def spread(q):
        part = act.at[q, me.c, me.y, 1 - me.h]
        send(part, part, az_s.at[q], az_r.at[q], mate).wait_recv()
        for k in (1, 2, 3):
            ay_copy(q, me.y, k).start()


    def ac_copy(q, c):
        part = act.at[q, c]
        return send(part, part, ac_s.at[q], ac_r.at[q], sib)

    def share(q):
        for k in (1, 2, 3):
            ay_copy(q, rem(me.y - k, NY), k).wait_recv()
        ac_copy(q, me.c).start()


    def e_copy(o):
        e = peer(o)
        return send(eo.at[e], rb.at[me.exp], e_s.at[o], e_r.at[me.exp], peer_dev(e))

    def down(q):
        x = src_x(q)
        ac_copy(q, 1 - me.c).wait_recv()
        value = jnp.dot(act[q, 0].reshape(128, HALF), wd_ref[0:HALF], preferred_element_type=F32)
        value += jnp.dot(act[q, 1].reshape(128, HALF), wd_ref[HALF:FF], preferred_element_type=F32)
        eo[pl.ds(x * NZ, NZ)] = value.astype(BF).reshape(NZ, 16, 256)

        def back(z):
            e_copy((NX - q) % NX * NZ + z).start()

        loop(NZ, back, 1 if q == 0 else 0)

    collect(1)
    gate_up(0)
    y_send(0)
    collect(2)
    gate_up(1)
    y_send(1)
    collect(3)
    gate_up(2)
    y_sum(0)
    y_send(2)
    gate_up(3)
    y_sum(1)
    y_send(3)
    y_sum(2)
    activate(0)
    y_sum(3)
    activate(1)
    activate(2)
    spread(0)
    activate(3)
    spread(1)
    share(0)
    spread(2)
    share(1)
    down(0)
    spread(3)
    share(2)
    down(1)
    share(3)
    down(2)
    down(3)
    rb[me.exp] = eo[me.exp]

    def chunk_left(q):
        a_copy(q).wait_send()
        z_copy(q).wait_send()
        az_copy(q).wait_send()
        ac_copy(q, me.c).wait_send()
        for k in (1, 2, 3):
            y_copy(q, k).wait_send()
            ay_copy(q, me.y, k).wait_send()

    loop(CH, chunk_left)
    loop(4 * NZ, d_left, 2 * NZ)

    def home(e):
        @pl.when(e != me.exp)
        def _():
            send(eo.at[0], rb.at[e], e_s.at[0], e_r.at[e], sib).wait_recv()

    loop(NX * NZ, home)
    back = rb[...].reshape(slots, 256)
    for half in range(2):
        got = jnp.dot(place_ref[half], back, preferred_element_type=F32)
        value = mixed[half].reshape(512, 256) + share_ref[half] * got
        out_ref[:, half] = value.astype(BF).reshape(NY, 128, 256)

    def e_left(o):
        e_copy(o).wait_send()

    loop(NX * NZ, e_left, 1)


def body(queries, new_kv, past_kv, residual, out_weight, norm_gain, routes, gates, w_gate_up, w_down):
    sem = pltpu.SemaphoreType.DMA
    wide = FF + EXT
    out = pl.pallas_call(
        layer_kernel,
        out_shape=jax.ShapeDtypeStruct((NY, 2, 128, 256), BF),
        in_specs=[pl.BlockSpec(memory_space=pl.ANY)] * 10,
        out_specs=pl.BlockSpec(memory_space=pltpu.VMEM),
        scratch_shapes=[
            pltpu.VMEM((CH, 16, D), BF),
            pltpu.VMEM((2, NY, 2, 2, 64, 512), BF),
            pltpu.VMEM((2, 32, 128, 256), BF),
            pltpu.VMEM((NY, 2, 2, CH, 16, 256), BF),
            pltpu.VMEM((1, 256), F32),
            pltpu.VMEM((16, 8, 64), jnp.int32),
            pltpu.VMEM((16, 8, 64), F32),
            pltpu.VMEM((256, 2 * FF), BF),
            pltpu.VMEM((FF, 256), BF),
            pltpu.VMEM((CH, 8, 16, D), BF),
            pltpu.VMEM((CH, KV_HEADS, 256, HEAD), F32),
            pltpu.VMEM((CH, KV_HEADS, 256, 1), F32),
            pltpu.VMEM((CH, KV_HEADS, 256, 1), F32),
            pltpu.VMEM((256, 1024), F32),
            pltpu.VMEM((CH, 128, 256), BF),
            pltpu.VMEM((CH, 128, 256), BF),
            pltpu.VMEM((2, NY, 2, CH, 16, 256), F32),
            pltpu.VMEM((2, 512, 512), BF),
            pltpu.VMEM((2, 512, 512), BF),
            pltpu.VMEM((2, 512, 1), F32),
            pltpu.VMEM((2, 8, 256), F32),
            pltpu.VMEM((256, FF), BF),
            pltpu.VMEM((512, 256), F32),
            pltpu.VMEM((32, 16, 256), BF),
            pltpu.VMEM((32, 16, 256), BF),
            pltpu.VMEM((32, 16, 256), BF),
            pltpu.VMEM((CH, 128, wide), BF),
            pltpu.VMEM((CH, 3, 32, wide), BF),
            pltpu.VMEM((CH, 32, wide), BF),
            pltpu.VMEM((CH, 16, wide), BF),
            pltpu.VMEM((CH, 2, NY, 2, 16, HALF), BF),
            pltpu.VMEM((32, 16, 256), BF),
            pltpu.VMEM((32, 16, 256), BF),
            sem((10,)),
            sem((30,)), sem((2, NY, 2, 2)),
            sem((2, 8)), sem((16,)),
            sem((4, 16)), sem((4, 16)),
            sem((CH, 8)), sem((CH, 8)), sem((CH, 2)),
            sem((CH,)), sem((CH,)),
            sem((3,)), sem((3,)),
            sem((32,)), sem((32,)),
            sem((4,)), sem((4,)),
            sem((CH, 3)), sem((CH, 3)),
            sem((CH,)), sem((CH,)),
            sem((CH,)), sem((CH,)),
            sem((CH, 3)), sem((CH, NY)),
            sem((CH,)), sem((CH,)),
            sem((32,)), sem((32,)),
        ],
        compiler_params=pltpu.CompilerParams(
            collective_id=0, has_side_effects=True, vmem_limit_bytes=56 * 2**20
        ),
        name="layer",
    )(
        queries.reshape(CH, 16, D),
        new_kv.reshape(64, 512),
        past_kv.reshape(64, 512),
        out_weight,
        residual.reshape(NY, 2, 2, CH, 16, 256),
        norm_gain.reshape(1, 256),
        jnp.swapaxes(routes.reshape(16, 64, 8), 1, 2),
        jnp.swapaxes(gates.reshape(16, 64, 8), 1, 2),
        w_gate_up.reshape(256, 2 * FF),
        w_down.reshape(FF, 256),
    )
    return out.reshape(16, 1, 64, 256)


def solution(mesh):
    in_specs = (
        P("ctx", "exp", None, None),
        P("ctx", "exp", None, None),
        P("ctx", "exp", None, None),
        P(None, "exp", None, "ctx"),
        P("exp", "ctx"),
        P("ctx"),
        P(None, "exp", None, None),
        P(None, "exp", None, None),
        P("exp", "ctx", None),
        P("exp", None, "ctx"),
    )
    return jax.shard_map(
        body, mesh=mesh, in_specs=in_specs, out_specs=P(None, "exp", None, "ctx"), check_vma=False
    )
```

```python
import math

import jax
import jax.numpy as jnp
from jax import lax
from jax.experimental import pallas as pl
from jax.experimental.pallas import tpu as pltpu
from jax.sharding import PartitionSpec as P

D = 4096
HEADS = 32
KV_HEADS = 2
HEAD = 128
FF = 1536
HALF = FF // 2
EXT = 128
NY, NX, NZ = 4, 4, 8
CH = 4
NEG = -1e30
SCALE = HEAD ** (-0.5) * math.log2(math.e)
BF = jnp.bfloat16
F32 = jnp.float32
MESH = pl.DeviceIdType.MESH


class Place:
    def __init__(self):
        ctx = lax.axis_index("ctx")
        exp = lax.axis_index("exp")
        self.y = lax.div(ctx, 4)
        self.h = lax.rem(lax.div(ctx, 2), 2)
        self.c = lax.rem(ctx, 2)
        self.x = lax.div(exp, NZ)
        self.z = lax.rem(exp, NZ)
        self.ctx = ctx
        self.exp = exp

    def dev(self, y=None, h=None, c=None, x=None, z=None):
        y = self.y if y is None else y
        h = self.h if h is None else h
        c = self.c if c is None else c
        x = self.x if x is None else x
        z = self.z if z is None else z
        return ((y * 2 + h) * 2 + c, x * NZ + z)


def rem(a, n):
    return lax.rem(a + n, n)


def send(src, dst, ss, rs, dev):
    return pltpu.make_async_remote_copy(
        src_ref=src, dst_ref=dst, send_sem=ss, recv_sem=rs, device_id=dev, device_id_type=MESH
    )


def greet(devs):
    barrier = pltpu.get_barrier_semaphore()
    for dev in devs:
        pl.semaphore_signal(barrier, inc=1, device_id=dev, device_id_type=MESH)


def loop(n, body, start=0):
    lax.fori_loop(start, n, lambda i, _: (body(i), None)[1], None)


def pieces(column, rows):
    lane = lax.broadcasted_iota(jnp.int32, (rows, EXT), 1)
    wide = jnp.broadcast_to(column, (rows, EXT))
    high = wide.astype(BF).astype(F32)
    rest = wide - high
    middle = rest.astype(BF).astype(F32)
    low = rest - middle
    out = jnp.where(lane == 0, high, jnp.where(lane == 1, middle, jnp.where(lane == 2, low, 0.0)))
    return out.astype(BF)


def layer_kernel(
    q_hbm, new_hbm, past_hbm, w_hbm, res_hbm, gain_hbm, routes_hbm, gates_hbm, gu_hbm, wd_hbm, out_ref,
    q_ref, kv, wb, res_ref, gain_ref, routes_ref, gates_ref, gu_ref, wd_ref,
    att, accs, tops, sums, s_ref, psend, precv, mixed, place_ref, place_t, share_ref,
    gains, wgs, picked, disp, arr, sarr, pb, yr, zb, zr, act, eo, rb,
    in_s, kv_s, kv_r, wz_s, wz_r, wx_s, wx_r, at_s, at_r, ah_r, p_s, p_r,
    c_s, c_r, d_s, d_r, a_s, a_r, y_s, y_r, z_s, z_r, az_s, az_r, ay_s, ay_r, ac_s, ac_r, e_s, e_r,
):
    me = Place()
    mate = me.dev(h=1 - me.h)
    sib = me.dev(c=1 - me.c)
    ring = me.h * NZ + me.z

    def ring_dev(step):
        there = rem(ring + step, 2 * NZ)
        return me.dev(h=lax.div(there, NZ), z=lax.rem(there, NZ))

    right, left = ring_dev(1), ring_dev(-1)
    ys = [me.dev(y=rem(me.y + k, NY)) for k in (1, 2, 3)]
    xs = [me.dev(x=rem(me.x + k, NX)) for k in (1, 2, 3)]

    def peer(o):
        x = rem(me.x + lax.div(o, NZ), NX)
        z = rem(me.z + lax.rem(o, NZ), NZ)
        return x * NZ + z

    def peer_dev(e):
        return (me.ctx, e)

    barrier = pltpu.get_barrier_semaphore()
    greet([mate, sib, right, left] + ys)

    def hello(o):
        pl.semaphore_signal(barrier, inc=1, device_id=peer_dev(peer(o)), device_id_type=MESH)

    loop(NX * NZ, hello, 1)

    pairs = [
        (past_hbm, kv.at[0, me.y, me.h, me.c]),
        (new_hbm, kv.at[1, me.y, me.h, me.c]),
        (w_hbm, wb.at[me.h, me.exp]),
        (routes_hbm, routes_ref),
        (gates_hbm, gates_ref),
        (q_hbm, q_ref),
        (gain_hbm, gain_ref),
        (gu_hbm, gu_ref),
        (wd_hbm, wd_ref),
        (res_hbm, res_ref),
    ]
    loads = [pltpu.make_async_copy(src, dst, in_s.at[i]) for i, (src, dst) in enumerate(pairs)]
    for load in loads:
        load.start()

    loads[3].wait()
    loads[4].wait()
    slots = 512
    step = 128
    tri = jnp.where(
        lax.broadcasted_iota(jnp.int32, (step, step), 1) < lax.broadcasted_iota(jnp.int32, (step, step), 0), 1.0, 0.0
    ).astype(BF)
    lane = lax.broadcasted_iota(jnp.int32, (step, 128), 1)
    slot = lax.broadcasted_iota(jnp.int32, (step, slots), 1)
    seen = jnp.zeros((1, 128), F32)

    def by_token(ref, t):
        return jnp.concatenate([ref[2 * t].T, ref[2 * t + 1].T], axis=0)

    for t in range(8):
        half, y = t % 2, t // 2
        routes = by_token(routes_ref, t)
        held = routes < NX * NZ
        target = jnp.sum(jnp.where(held, routes, 0), axis=1, keepdims=True)
        has = jnp.sum(jnp.where(held, 1, 0), axis=1, keepdims=True)
        share_ref[half, y * step : (y + 1) * step] = jnp.sum(
            jnp.where(held, by_token(gates_ref, t), 0.0), axis=1, keepdims=True
        )
        named = jnp.where(has > 0, target, -1)
        part = jnp.where(lane == named, 1.0, 0.0)
        before = jnp.dot(tri, part.astype(BF), preferred_element_type=F32) + seen
        at = jnp.sum(before * part, axis=1, keepdims=True).astype(jnp.int32)
        index = jnp.where(named >= 0, named * 16 + at, -1)
        hot = jnp.where(slot == index, 1.0, 0.0)
        place_ref[half, y * step : (y + 1) * step] = hot.astype(BF)
        place_t[half, :, y * step : (y + 1) * step] = hot.T.astype(BF)
        seen = seen + jnp.sum(part, axis=0, keepdims=True)

    for i in (0, 1, 2):
        loads[i].wait()
    pl.semaphore_wait(barrier, 38)

    def kv_copy(n, y, h, c, out, dev):
        part = kv.at[n, y, h, c]
        return send(part, part, kv_s.at[out], kv_r.at[n, y, h, c], dev)

    kv_copies = []

    def kv_go(n, y, h, c, dev):
        copy = kv_copy(n, y, h, c, len(kv_copies), dev)
        copy.start()
        kv_copies.append(copy)

    def kv_wait(n, y, h, c):
        kv_copy(n, y, h, c, 0, sib).wait_recv()

    for n in range(2):
        kv_go(n, me.y, me.h, me.c, mate)
    for n in range(2):
        for k in (0, 2, 1):
            kv_go(n, me.y, me.h, me.c, ys[k])
        kv_go(n, me.y, me.h, me.c, sib)

    def w_part(shard, x):
        return wb.at[lax.div(shard, NZ), x * NZ + lax.rem(shard, NZ)]

    def w_right(s):
        shard = rem(ring - s + 1, 2 * NZ)
        part = w_part(shard, me.x)
        return send(part, part, wz_s.at[0, s - 1], wz_r.at[shard], right)

    def w_left(s):
        shard = rem(ring + s - 1, 2 * NZ)
        part = w_part(shard, me.x)
        return send(part, part, wz_s.at[1, s - 1], wz_r.at[shard], left)

    def w_wait(shard):
        part = w_part(shard, me.x)
        send(part, part, wz_s.at[0, 0], wz_r.at[shard], right).wait_recv()

    x_up, x_down = xs[0], xs[2]

    def w_x(shard, i):
        if i < 2:
            part = w_part(shard, me.x)
        else:
            part = w_part(shard, rem(me.x + 2 * i - 5, NX)).at[pl.ds((i - 2) * 64, 64)]
        return send(part, part, wx_s.at[i, shard], wx_r.at[i, shard], (x_up, x_down)[i % 2])

    def w_x_wait(shard, i):
        part = w_part(shard, rem(me.x + (-1, 1, 2, 2)[i], NX))
        if i >= 2:
            part = part.at[pl.ds((i - 2) * 64, 64)]
        send(part, part, wx_s.at[i, shard], wx_r.at[i, shard], x_up).wait_recv()

    def w_spread(shard):
        for i in (0, 1):
            w_x(shard, i).start()

    def w_pass(shard):
        for i in (0, 1):
            w_x_wait(shard, i)
            w_x(shard, i + 2).start()

    def ring_send(s):
        w_right(s).start()

        @pl.when(s < NZ)
        def _():
            w_left(s).start()

    def ring_take(s):
        one = rem(ring - s, 2 * NZ)
        w_wait(one)

        @pl.when(s < NZ)
        def _():
            w_wait(rem(ring + s, 2 * NZ))

    def both(s, act_on):
        act_on(rem(ring - s, 2 * NZ))

        @pl.when(s < NZ)
        def _():
            act_on(rem(ring + s, 2 * NZ))

    def ring_step(s):
        ring_take(s)

        @pl.when(s < NZ)
        def _():
            ring_send(s + 1)

        both(s, w_spread)

    ring_send(1)
    w_spread(ring)
    for n in range(2):
        for k in (1, 3, 2):
            y = rem(me.y - k, NY)
            kv_wait(n, y, me.h, me.c)
            kv_go(n, y, me.h, me.c, sib)
    ring_step(1)
    for n in range(2):
        for y in range(NY):
            kv_wait(n, y, me.h, 1 - me.c)
    loads[5].wait()

    mine = me.y * 2 + me.c
    tok = 16
    keys = 512
    per = HEADS // KV_HEADS
    row = lax.broadcasted_iota(jnp.int32, (tok, keys), 0)
    col = lax.broadcasted_iota(jnp.int32, (tok, keys), 1)

    def attend(chunk, half, first):
        spot = lax.div(col, 128) * 256 + half * 128 + lax.rem(col, 128)
        bias = jnp.where(spot <= row + (me.ctx * 64 + chunk * tok), 0.0, NEG)
        for g in range(KV_HEADS):
            q = jnp.concatenate(
                [q_ref[chunk, :, (g * per + i) * HEAD : (g * per + i + 1) * HEAD] for i in range(per)], axis=0
            )
            top = None if first else tops[chunk, g]
            for kt in range(2):
                k = kv[kt, :, half, :, :, g * HEAD : (g + 1) * HEAD].reshape(keys, HEAD)
                s = lax.dot_general(q, k, (((1,), (1,)), ((), ())), preferred_element_type=F32)
                if kt == 1:
                    s = (s.reshape(per, tok, keys) + bias[None]).reshape(per * tok, keys)
                s_ref[:, kt * keys : (kt + 1) * keys] = s
                m = jnp.max(s, axis=1, keepdims=True)
                top = m if top is None else jnp.maximum(top, m)
            total = None
            acc = None
            for kt in range(2):
                p = jnp.exp2((s_ref[:, kt * keys : (kt + 1) * keys] - top) * SCALE)
                v = kv[kt, :, half, :, :, (KV_HEADS + g) * HEAD : (KV_HEADS + g + 1) * HEAD].reshape(keys, HEAD)
                t = jnp.sum(p, axis=1, keepdims=True)
                o = jnp.dot(p.astype(BF), v, preferred_element_type=F32)
                total = t if total is None else total + t
                acc = o if acc is None else acc + o
            if first:
                tops[chunk, g] = top
                sums[chunk, g] = total
                accs[chunk, g] = acc
            else:
                fade = jnp.exp2((tops[chunk, g] - top) * SCALE)
                total = total + sums[chunk, g] * fade
                acc = acc + accs[chunk, g] * fade
                out = (acc / total).astype(BF)
                for i in range(per):
                    att[chunk, mine, :, (g * per + i) * HEAD : (g * per + i + 1) * HEAD] = out[
                        i * tok : (i + 1) * tok
                    ]

    def first_half(chunk):
        attend(chunk, me.h, True)

        @pl.when(lax.rem(chunk, 2) == 1)
        def _():
            ring_step(2 + lax.div(chunk, 2))

    loop(CH, first_half)
    w_pass(ring)

    for n in range(2):
        kv_wait(n, me.y, 1 - me.h, me.c)
        for k in (0, 2, 1):
            kv_go(n, me.y, 1 - me.h, me.c, ys[k])
        kv_go(n, me.y, 1 - me.h, me.c, sib)
    ring_step(4)
    both(1, w_pass)

    loads[6].wait()
    loads[7].wait()
    gains[me.c] = jnp.broadcast_to(gain_ref[...], (8, 256))
    theirs = pl.multiple_of((1 - me.c) * HALF, 128)
    c_copies = [
        send(gu_ref.at[:, pl.ds(theirs, HALF)], wgs.at[:, pl.ds(0, HALF)], c_s.at[0], c_r.at[0], sib),
        send(gu_ref.at[:, pl.ds(theirs + FF, HALF)], wgs.at[:, pl.ds(HALF, HALF)], c_s.at[1], c_r.at[1], sib),
        send(gains.at[me.c], gains.at[me.c], c_s.at[2], c_r.at[2], sib),
    ]
    for n in range(2):
        for k in (1, 3, 2):
            y = rem(me.y - k, NY)
            kv_wait(n, y, 1 - me.h, me.c)
            kv_go(n, y, 1 - me.h, me.c, sib)
    ring_step(5)
    both(2, w_pass)
    for n in range(2):
        for y in range(NY):
            kv_wait(n, y, 1 - me.h, 1 - me.c)
    for copy in c_copies:
        copy.start()

    def who(k):
        return rem(me.y + k, NY) * 2 + me.c

    def att_full(chunk, w, out, dev):
        part = att.at[chunk, w]
        return send(part, part, at_s.at[chunk, out], at_r.at[chunk, w], dev)

    def att_half(chunk, w, part, out, dev):
        cols = att.at[chunk, w, :, pl.ds(part * (D // 2), D // 2)]
        return send(cols, cols, at_s.at[chunk, out], ah_r.at[chunk, part], dev)

    up, down_y = ys[0], ys[2]

    def att_send(chunk, i):
        if i < 3:
            return att_full(chunk, mine, i, (up, down_y, sib)[i])
        if i < 5:
            return att_half(chunk, who((-1, 1)[i - 3]), i - 3, i, (up, down_y)[i - 3])
        return att_full(chunk, who((-1, 1, 2)[i - 5]), i, sib)

    def pass_on(chunk):
        att_full(chunk, who(-1), 0, up).wait_recv()
        att_send(chunk, 3).start()
        att_full(chunk, who(1), 0, up).wait_recv()
        for i in (4, 5, 6):
            att_send(chunk, i).start()

    def pass_last(chunk):
        att_half(chunk, who(2), 0, 0, up).wait_recv()
        att_half(chunk, who(2), 1, 0, up).wait_recv()
        att_send(chunk, 7).start()

    def second_half(chunk):
        attend(chunk, 1 - me.h, False)
        for i in range(3):
            att_send(chunk, i).start()

        @pl.when(chunk < 3)
        def _():
            ring_step(6 + chunk)

        both(chunk + 3, w_pass)

        @pl.when(chunk > 0)
        def _():
            pass_on(chunk - 1)

        @pl.when(chunk > 1)
        def _():
            pass_last(chunk - 2)

    loop(CH, second_half)

    def w_arrive(half):
        def one(z):
            shard = half * NZ + z
            for i in (2, 3):
                w_x_wait(shard, i)

        loop(NZ, one)

    both(NZ - 1, w_pass)
    w_pass(rem(ring - NZ, 2 * NZ))
    w_arrive(1 - me.h)

    def p_copy(chunk):
        return send(psend.at[chunk], precv.at[chunk], p_s.at[chunk], p_r.at[chunk], mate)

    def rows_of(chunk):
        return att[chunk].reshape(8 * tok, D)

    def for_mate(chunk):
        for y in range(NY):
            att_full(chunk, y * 2 + 1 - me.c, 0, sib).wait_recv()
        psend[chunk] = jnp.dot(rows_of(chunk), wb[1 - me.h].reshape(D, 256), preferred_element_type=F32).astype(BF)
        p_copy(chunk).start()

    for_mate(0)
    pass_on(CH - 1)
    for_mate(1)
    pass_last(CH - 2)
    for_mate(2)
    pass_last(CH - 1)
    for_mate(3)
    w_arrive(me.h)
    loads[9].wait()

    def put(chunk, half, value):
        for j in range(8):
            y, c = j // 2, j % 2
            mixed[half, y, c, chunk] = res_ref[y, half, c, chunk].astype(F32) + value[j * tok : (j + 1) * tok].astype(
                F32
            )

    def for_me(chunk):
        put(chunk, me.h, jnp.dot(rows_of(chunk), wb[me.h].reshape(D, 256), preferred_element_type=F32))

    loop(CH, for_me)

    def pick(half):
        rows = (mixed[half].reshape(512, 256) * gain_ref[...]).astype(BF)
        return jnp.dot(place_t[half], rows, preferred_element_type=F32)

    picked[...] = pick(me.h)

    def from_mate(chunk):
        p_copy(chunk).wait_recv()
        put(chunk, 1 - me.h, precv[chunk])

    loop(CH, from_mate)
    disp[...] = (picked[...] + pick(1 - me.h)).astype(BF).reshape(32, 16, 256)

    def d_copy(o):
        e = peer(o)
        return send(disp.at[e], arr.at[me.exp], d_s.at[o], d_r.at[me.exp], peer_dev(e))

    def d_start(o):
        d_copy(o).start()

    def d_left(o):
        d_copy(o).wait_send()

    loop(2 * NZ, d_start, 1)
    arr[me.exp] = disp[me.exp]
    loop(NZ, d_left, 1)
    loop(3 * NZ, d_start, 2 * NZ)
    loop(2 * NZ, d_left, NZ)
    loop(4 * NZ, d_start, 3 * NZ)
    def src_x(q):
        return rem(me.x - q, NX)

    def a_copy(q):
        x = src_x(q)
        part = arr.at[pl.ds(x * NZ, NZ)]
        return send(part, sarr.at[pl.ds(x * NZ, NZ)], a_s.at[x], a_r.at[x], sib)

    def collect(q):
        x = src_x(q)

        def one(z):
            e = x * NZ + z

            @pl.when(e != me.exp)
            def _():
                send(disp.at[0], arr.at[e], d_s.at[0], d_r.at[e], sib).wait_recv()

        loop(NZ, one)
        a_copy(q).start()

    for copy in c_copies + kv_copies:
        copy.wait_send()

    def ring_left(s):
        w_right(s).wait_send()

        @pl.when(s < NZ)
        def _():
            w_left(s).wait_send()

    loop(NZ + 1, ring_left, 1)

    def x_left(shard):
        for i in range(4):
            w_x(shard, i).wait_send()

    loop(2 * NZ, x_left)

    def att_left(q):
        for i in range(8):
            att_send(q, i).wait_send()
        p_copy(q).wait_send()

    loop(CH, att_left)
    collect(0)
    loads[8].wait()
    c_copies[0].wait_recv()
    c_copies[1].wait_recv()
    send(gains.at[me.c], gains.at[1 - me.c], c_s.at[2], c_r.at[2], sib).wait_recv()
    ours = pl.multiple_of(me.c * HALF, 128)

    def y_copy(q, k):
        there = rem(me.y + k, NY)
        part = pb.at[q, pl.ds(there * 32, 32)]
        return send(part, yr.at[q, k - 1], y_s.at[q, k - 1], y_r.at[q, k - 1], ys[k - 1])

    def gate_up(q):
        x = src_x(q)
        a_copy(q).wait_recv()
        mine = arr[pl.ds(x * NZ, NZ)].reshape(128, 256)
        other = sarr[pl.ds(x * NZ, NZ)].reshape(128, 256)
        a = mine.astype(F32) / gains[me.c, 0:1]
        b = other.astype(F32) / gains[1 - me.c, 0:1]
        squares = jnp.sum(a * a, axis=1, keepdims=True) + jnp.sum(b * b, axis=1, keepdims=True)
        pb[q, :, FF * 1 :] = pieces(squares, 128)
        gate = jnp.dot(mine, gu_ref[:, pl.ds(ours, HALF)], preferred_element_type=F32)
        gate += jnp.dot(other, wgs[:, 0:HALF], preferred_element_type=F32)
        pb[q, :, 0:HALF] = gate.astype(BF)
        up = jnp.dot(mine, gu_ref[:, pl.ds(ours + FF, HALF)], preferred_element_type=F32)
        up += jnp.dot(other, wgs[:, HALF:FF], preferred_element_type=F32)
        pb[q, :, HALF:FF] = up.astype(BF)

    def y_send(q):
        for k in (1, 3, 2):
            y_copy(q, k).start()

    def z_copy(q):
        part = zb.at[q, pl.ds((1 - me.h) * 16, 16)]
        return send(part, zr.at[q], z_s.at[q], z_r.at[q], mate)

    def y_sum(q):
        total = pb[q, pl.ds(pl.multiple_of(me.y * 32, 32), 32)].astype(F32)
        for k in (1, 2, 3):
            y_copy(q, k).wait_recv()
            total = total + yr[q, k - 1].astype(F32)
        zb[q, :, 0:FF] = total[:, 0:FF].astype(BF)
        zb[q, :, FF:] = pieces(jnp.sum(total[:, FF:], axis=1, keepdims=True), 32)
        z_copy(q).start()


    def az_copy(q):
        part = act.at[q, me.c, me.y, me.h]
        return send(part, part, az_s.at[q], az_r.at[q], mate)

    def activate(q):
        z_copy(q).wait_recv()
        total = zb[q, pl.ds(pl.multiple_of(me.h * 16, 16), 16)].astype(F32) + zr[q].astype(F32)
        squares = jnp.sum(total[:, FF:], axis=1, keepdims=True)
        scale = lax.rsqrt(squares / D + 1e-6)
        gate = total[:, 0:HALF] * scale
        up = total[:, HALF:FF] * scale
        act[q, me.c, me.y, me.h] = (gate / (1.0 + jnp.exp(-gate)) * up).astype(BF)
        az_copy(q).start()


    def ay_copy(q, y, k):
        part = act.at[q, me.c, y]
        return send(part, part, ay_s.at[q, k - 1], ay_r.at[q, y], ys[k - 1])

    def spread(q):
        part = act.at[q, me.c, me.y, 1 - me.h]
        send(part, part, az_s.at[q], az_r.at[q], mate).wait_recv()
        for k in (1, 2, 3):
            ay_copy(q, me.y, k).start()


    def ac_copy(q, c):
        part = act.at[q, c]
        return send(part, part, ac_s.at[q], ac_r.at[q], sib)

    def share(q):
        for k in (1, 2, 3):
            ay_copy(q, rem(me.y - k, NY), k).wait_recv()
        ac_copy(q, me.c).start()


    def e_copy(o):
        e = peer(o)
        return send(eo.at[e], rb.at[me.exp], e_s.at[o], e_r.at[me.exp], peer_dev(e))

    def down(q):
        x = src_x(q)
        ac_copy(q, 1 - me.c).wait_recv()
        value = jnp.dot(act[q, 0].reshape(128, HALF), wd_ref[0:HALF], preferred_element_type=F32)
        value += jnp.dot(act[q, 1].reshape(128, HALF), wd_ref[HALF:FF], preferred_element_type=F32)
        eo[pl.ds(x * NZ, NZ)] = value.astype(BF).reshape(NZ, 16, 256)

        def back(z):
            e_copy((NX - q) % NX * NZ + z).start()

        loop(NZ, back, 1 if q == 0 else 0)

    collect(1)
    gate_up(0)
    y_send(0)
    collect(2)
    gate_up(1)
    y_send(1)
    collect(3)
    gate_up(2)
    y_sum(0)
    y_send(2)
    gate_up(3)
    y_sum(1)
    y_send(3)
    y_sum(2)
    activate(0)
    y_sum(3)
    activate(1)
    activate(2)
    spread(0)
    activate(3)
    spread(1)
    share(0)
    spread(2)
    share(1)
    down(0)
    spread(3)
    share(2)
    down(1)
    share(3)
    down(2)
    down(3)
    rb[me.exp] = eo[me.exp]

    def chunk_left(q):
        a_copy(q).wait_send()
        z_copy(q).wait_send()
        az_copy(q).wait_send()
        ac_copy(q, me.c).wait_send()
        for k in (1, 2, 3):
            y_copy(q, k).wait_send()
            ay_copy(q, me.y, k).wait_send()

    loop(CH, chunk_left)
    loop(4 * NZ, d_left, 2 * NZ)

    def home(e):
        @pl.when(e != me.exp)
        def _():
            send(eo.at[0], rb.at[e], e_s.at[0], e_r.at[e], sib).wait_recv()

    loop(NX * NZ, home)
    back = rb[...].reshape(slots, 256)
    for half in range(2):
        got = jnp.dot(place_ref[half], back, preferred_element_type=F32)
        value = mixed[half].reshape(512, 256) + share_ref[half] * got
        out_ref[:, half] = value.astype(BF).reshape(NY, 128, 256)

    def e_left(o):
        e_copy(o).wait_send()

    loop(NX * NZ, e_left, 1)


def body(queries, new_kv, past_kv, residual, out_weight, norm_gain, routes, gates, w_gate_up, w_down):
    sem = pltpu.SemaphoreType.DMA
    wide = FF + EXT
    out = pl.pallas_call(
        layer_kernel,
        out_shape=jax.ShapeDtypeStruct((NY, 2, 128, 256), BF),
        in_specs=[pl.BlockSpec(memory_space=pl.ANY)] * 10,
        out_specs=pl.BlockSpec(memory_space=pltpu.VMEM),
        scratch_shapes=[
            pltpu.VMEM((CH, 16, D), BF),
            pltpu.VMEM((2, NY, 2, 2, 64, 512), BF),
            pltpu.VMEM((2, 32, 128, 256), BF),
            pltpu.VMEM((NY, 2, 2, CH, 16, 256), BF),
            pltpu.VMEM((1, 256), F32),
            pltpu.VMEM((16, 8, 64), jnp.int32),
            pltpu.VMEM((16, 8, 64), F32),
            pltpu.VMEM((256, 2 * FF), BF),
            pltpu.VMEM((FF, 256), BF),
            pltpu.VMEM((CH, 8, 16, D), BF),
            pltpu.VMEM((CH, KV_HEADS, 256, HEAD), F32),
            pltpu.VMEM((CH, KV_HEADS, 256, 1), F32),
            pltpu.VMEM((CH, KV_HEADS, 256, 1), F32),
            pltpu.VMEM((256, 1024), F32),
            pltpu.VMEM((CH, 128, 256), BF),
            pltpu.VMEM((CH, 128, 256), BF),
            pltpu.VMEM((2, NY, 2, CH, 16, 256), F32),
            pltpu.VMEM((2, 512, 512), BF),
            pltpu.VMEM((2, 512, 512), BF),
            pltpu.VMEM((2, 512, 1), F32),
            pltpu.VMEM((2, 8, 256), F32),
            pltpu.VMEM((256, FF), BF),
            pltpu.VMEM((512, 256), F32),
            pltpu.VMEM((32, 16, 256), BF),
            pltpu.VMEM((32, 16, 256), BF),
            pltpu.VMEM((32, 16, 256), BF),
            pltpu.VMEM((CH, 128, wide), BF),
            pltpu.VMEM((CH, 3, 32, wide), BF),
            pltpu.VMEM((CH, 32, wide), BF),
            pltpu.VMEM((CH, 16, wide), BF),
            pltpu.VMEM((CH, 2, NY, 2, 16, HALF), BF),
            pltpu.VMEM((32, 16, 256), BF),
            pltpu.VMEM((32, 16, 256), BF),
            sem((10,)),
            sem((30,)), sem((2, NY, 2, 2)),
            sem((2, 8)), sem((16,)),
            sem((4, 16)), sem((4, 16)),
            sem((CH, 8)), sem((CH, 8)), sem((CH, 2)),
            sem((CH,)), sem((CH,)),
            sem((3,)), sem((3,)),
            sem((32,)), sem((32,)),
            sem((4,)), sem((4,)),
            sem((CH, 3)), sem((CH, 3)),
            sem((CH,)), sem((CH,)),
            sem((CH,)), sem((CH,)),
            sem((CH, 3)), sem((CH, NY)),
            sem((CH,)), sem((CH,)),
            sem((32,)), sem((32,)),
        ],
        compiler_params=pltpu.CompilerParams(
            collective_id=0, has_side_effects=True, vmem_limit_bytes=56 * 2**20
        ),
        name="layer",
    )(
        queries.reshape(CH, 16, D),
        new_kv.reshape(64, 512),
        past_kv.reshape(64, 512),
        out_weight,
        residual.reshape(NY, 2, 2, CH, 16, 256),
        norm_gain.reshape(1, 256),
        jnp.swapaxes(routes.reshape(16, 64, 8), 1, 2),
        jnp.swapaxes(gates.reshape(16, 64, 8), 1, 2),
        w_gate_up.reshape(256, 2 * FF),
        w_down.reshape(FF, 256),
    )
    return out.reshape(16, 1, 64, 256)


def solution(mesh):
    in_specs = (
        P("ctx", "exp", None, None),
        P("ctx", "exp", None, None),
        P("ctx", "exp", None, None),
        P(None, "exp", None, "ctx"),
        P("exp", "ctx"),
        P("ctx"),
        P(None, "exp", None, None),
        P(None, "exp", None, None),
        P("exp", "ctx", None),
        P("exp", None, "ctx"),
    )
    return jax.shard_map(
        body, mesh=mesh, in_specs=in_specs, out_specs=P(None, "exp", None, "ctx"), check_vma=False
    )
```
